256 devices in a mesh: sx: 8 (over x, y_lo), sy: 32 (over z, y_hi, core).
Axes of the slice: x: 4, y: 4 (y_hi: 2, y_lo: 2; y = y_hi * 2 + y_lo), z: 8, core: 2. Of those that a mesh axis runs over, the one named last changes fastest.
Arguments:
- volume: bfloat16 [16, 32, 256, 256], P('sx', None, 'sy'), may hold values from -6 to 6
- kernel_one: bfloat16 [32, 32, 3, 3, 3], replicated, may hold values from -0.21875 to 0.21875
- bias_one: bfloat16 [32], replicated, may hold values from -3 to 3
- kernel_two: bfloat16 [64, 32, 3, 3, 3], replicated, may hold values from -0.21875 to 0.21875
- out_grad: bfloat16 [8, 64, 128, 128], P(None, 'sx', 'sy'), may hold values from -12 to 12
Outputs:
- strided_out: bfloat16 [8, 64, 128, 128], P(None, 'sx', 'sy')
- grad_two: float32 [64, 32, 3, 3, 3], P('sx')
- grad_one: float32 [32, 32, 3, 3, 3], replicated
- grad_volume: bfloat16 [16, 32, 256, 256], P('sx', None, 'sy')
The draws below stay inside these ranges and needn't reach their ends.
All inputs are finite; a program needn't handle non-finite values.
Results may differ from the reference program's by a relative error of at most 0.005.
Values may be sent and summed in bfloat16 or wider, within the bound.
No kernel may reach another device: no remote copies, remote signals or barrier semaphores. Data moves between devices by JAX's collectives and lax.ppermute only.
A program may use at most 128 MiB of HBM per device.

```python
import jax
import jax.numpy as jnp
from jax import lax

C = 32
K = 64
W = 256
ND = 16
NH = 256
D2 = 8
H2 = 128
W2 = 128


def levels(rng, dims, split, low, high):
    def one(axis_at, blocks):
        draws = jax.random.uniform(jax.random.fold_in(jax.random.fold_in(rng, 6), axis_at), (blocks,), jnp.float32, low / len(split), high / len(split))
        return jnp.repeat(jnp.exp(draws), dims[axis_at] // blocks).reshape((-1,) + (1,) * (len(dims) - axis_at - 1))

    loudness = one(*split[0])
    for cut in split[1:]:
        loudness = loudness * one(*cut)
    return loudness


def noise(key, dims, width, bound, cuts=(), kind=jnp.bfloat16):
    values = jax.random.normal(key, dims, jnp.float32) * width
    if len(cuts) > 0:
        values = levels(key, dims, cuts, -0.22, 0.18) * values
    return jnp.clip(values, min=-bound, max=bound).astype(kind)


def setup_inputs(seed: int = 0) -> dict:
    key_of = jax.random.split(jax.random.key(seed), 6)
    volume = noise(key_of[0], (ND, C, NH, W), 1.0, 6.0, ((0, 8), (2, 32)))
    kernel_one = noise(key_of[1], (C, C, 3, 3, 3), (27 * C) ** -0.5, 0.21875)
    bias_one = noise(key_of[2], (C,), 0.5, 3.0)
    kernel_two = noise(key_of[3], (K, C, 3, 3, 3), (27 * C) ** -0.5, 0.21875)
    out_grad = noise(key_of[4], (D2, K, H2, W2), 3.0, 12.0, ((1, 8), (2, 32)))
    return dict(volume=volume, kernel_one=kernel_one, bias_one=bias_one, kernel_two=kernel_two, out_grad=out_grad)


def conv_full(lhs, rhs, strides):
    pads = ((1, 1), (1, 1), (1, 1))
    return lax.conv_general_dilated(lhs[None], rhs, strides, pads, dimension_numbers=('NDCHW', 'OIDHW', 'NDCHW'), precision=lax.Precision.HIGHEST)[0]

def reference(volume, kernel_one, bias_one, kernel_two, out_grad):
    volume_f = volume.astype(jnp.float32)
    kernel_one_f = kernel_one.astype(jnp.float32)
    kernel_two_f = kernel_two.astype(jnp.float32)

    def layer_one(inputs, weights):
        return conv_full(inputs, weights, (1, 1, 1))

    def layer_two(inputs, weights):
        return conv_full(inputs, weights, (2, 2, 2))
    pre = layer_one(volume_f, kernel_one_f) + bias_one.astype(jnp.float32)[None, :, None, None]
    act = jax.nn.silu(pre).astype(jnp.bfloat16)
    strided, back_two = jax.vjp(layer_two, act.astype(jnp.float32), kernel_two_f)
    grad_act, grad_two = back_two(out_grad.astype(jnp.float32))
    sigma = jax.nn.sigmoid(pre)
    grad_pre = (grad_act * sigma * (1.0 + pre * (1.0 - sigma))).astype(jnp.bfloat16)
    unused, back_one = jax.vjp(layer_one, volume_f, kernel_one_f)
    grad_volume, grad_one = back_one(grad_pre.astype(jnp.float32))
    out_scale = (D2 * H2 * W2) ** (-0.5)
    in_scale = (ND * NH * W) ** (-0.5)
    return (strided.astype(jnp.bfloat16), grad_two * out_scale, grad_one * in_scale, grad_volume.astype(jnp.bfloat16))
```

```python
import functools

import jax
import jax.numpy as jnp
import numpy as np
from jax import lax
from jax.experimental import pallas as pl
from jax.experimental.pallas import tpu as pltpu
from jax.sharding import PartitionSpec as P

F32 = jnp.float32
BF16 = jnp.bfloat16
NX = 8
NY = 32
C = 32
K = 64
W = 256
CLASSES = ((0, 0), (0, 1), (1, 0), (1, 1))
TAPS = tuple((a, c) for a in range(3) for c in range(3))
VMEM = 48 * 1024 * 1024


def row_order(outer, middle, inner):
    n = outer * middle * inner
    m = np.zeros((n, n), np.float32)
    for o in range(outer):
        for a in range(middle):
            for b in range(inner):
                m[(o * inner + b) * middle + a, (o * middle + a) * inner + b] = 1
    return m


def spread_columns():
    m = np.zeros((640, NX * 128), np.float32)
    for j in range(NX):
        for u in range(18):
            for pd, pw in CLASSES:
                w = 32 * j - 2 + 2 * u + pw
                if 0 <= w < W:
                    m[pd * W + w, j * 128 + (pd * 2 + pw) * 20 + u] = 1
            g = 16 * j - 1 + u
            if 0 <= g < 128:
                m[512 + g, j * 128 + 80 + u] = 1
    return m


def class_columns():
    m = np.zeros((512, 512), np.float32)
    for s in range(4):
        for cls in range(4):
            for u in range(18):
                m[s * 128 + cls * 20 + u, cls * 128 + s * 32 + u] = 1
    return m


def cotangent_columns():
    m = np.zeros((1024, 256), np.float32)
    for e in range(8):
        for u in range(18):
            m[e * 128 + 80 + u, e * 32 + u] = 1
    return m


def strided_columns():
    m = np.zeros((256, 128), np.float32)
    for e in range(8):
        for u in range(16):
            m[e * 32 + 1 + u, e * 16 + u] = 1
    return m


def gather_columns():
    m = np.zeros((1024, 512), np.float32)
    for half in range(2):
        for cls in range(4):
            for e in range(4):
                for u in range(16):
                    m[half * 512 + cls * 128 + e * 32 + 1 + u, e * 128 + half * 64 + cls * 16 + u] = 1
    return m


def plane_columns():
    m = np.zeros((512, 512), np.float32)
    for j in range(4):
        for half in range(2):
            for pd, pw in CLASSES:
                for u in range(16):
                    row = j * 128 + half * 64 + (pd * 2 + pw) * 16 + u
                    m[row, (pd * 2 + half) * 128 + 32 * j + 2 * u + pw] = 1
    return m


def strided_planes():
    m = np.zeros((1024, 1024), np.float32)
    for j in range(8):
        for e in range(8):
            for u in range(16):
                m[j * 128 + e * 16 + u, e * 128 + j * 16 + u] = 1
    return m


def kernel_rows():
    m = np.zeros((320, 288), np.float32)
    for s in range(8):
        for t in range(9):
            for o in range(4):
                m[s * 40 + t * 4 + o, t * 32 + 4 * s + o] = 1
    return m


def const(m):
    return jnp.asarray(m, BF16)


def dot(a, b):
    return jnp.dot(a, b, preferred_element_type=F32)


def move(a, b):
    return dot(a, b).astype(BF16)


def dot_nt(a, b):
    return lax.dot_general(a, b, (((1,), (1,)), ((), ())), preferred_element_type=F32)


def ahead(x, n):
    return jnp.concatenate([x[:, n:], jnp.zeros((x.shape[0], n), x.dtype)], axis=1)


def behind(x, n):
    return jnp.concatenate([jnp.zeros((x.shape[0], n), x.dtype), x[:, :-n]], axis=1)


def step(parity, offset):
    at = parity + offset
    return (1, 1) if at == -1 else (0, 1) if at == 2 else (at, 0)


def variant(pd, pw, da, dc):
    qd, sd = step(pd, da)
    qw, sw = step(pw, dc)
    return ((qd * 2 + qw) * 2 + sd) * 2 + sw


def store_variants(ref, x, cls):
    pd, pw = cls
    base = (pd * 2 + pw) * 4
    move_d = behind if pd else ahead
    move_w = behind if pw else ahead
    along = move_w(x, 1)
    ref[base] = x
    ref[base + 1] = along
    ref[base + 2] = move_d(x, 32)
    ref[base + 3] = move_d(along, 32)


def pack_kernel(vol_ref, og_ref, rows_ref, og_rows_ref, cols_ref, out_ref):
    rows = rows_ref[...]
    v0 = move(rows, vol_ref[0:256])
    v1 = move(rows, vol_ref[256:512])
    og = move(og_rows_ref[...], og_ref[...])
    cat = jnp.concatenate([v0, v1, og], axis=1)
    for j in range(NX):
        out_ref[j] = move(cat, cols_ref[:, j * 128 : (j + 1) * 128])


def unpack_kernel(r_ref, cls_ref, og_cols_ref, x_ref, og_ref, up_ref, down_ref):
    for q in range(2):
        cat = jnp.concatenate([r_ref[4 * q + s] for s in range(4)], axis=1)
        got = move(cat, cls_ref[...])
        for cls in range(4):
            at = slice(cls * 256 + q * 128, cls * 256 + (q + 1) * 128)
            part = got[:, cls * 128 : (cls + 1) * 128]
            x_ref[:, at] = part
            up_ref[:, at] = part[192:256]
            down_ref[:, at] = part[0:64]
    parts = []
    for s in range(NX):
        parts.append(jnp.concatenate([r_ref[s, e * 32 : (e + 1) * 32, :] for e in range(8)], axis=1))
    og = dot(jnp.concatenate(parts, axis=0), og_cols_ref[...])
    og = jnp.concatenate(
        [og[s * 32 + g * 8 : s * 32 + g * 8 + 8] for g in range(4) for s in range(NX)], axis=0
    ).astype(BF16)
    og_ref[...] = og
    up_ref[:, 1024:1280] = og[192:256]
    down_ref[:, 1024:1280] = og[0:64]


def place(strip, offset, width):
    parts = [strip]
    if offset:
        parts.insert(0, jnp.zeros((strip.shape[0], offset), strip.dtype))
    rest = width - offset - strip.shape[1]
    if rest:
        parts.append(jnp.zeros((strip.shape[0], rest), strip.dtype))
    return jnp.concatenate(parts, axis=1)


def weights_kernel(k1_ref, k2_ref, t1_ref, t1t_ref, t2_ref, t2t_ref):
    for t, (a, c) in enumerate(TAPS):
        k1 = [k1_ref[a * 9 + b * 3 + c].astype(F32) for b in range(3)]
        k2 = [k2_ref[a * 9 + b * 3 + c].astype(F32) for b in range(3)]
        forward = jnp.concatenate(k1, axis=1)
        back = jnp.concatenate([x.T for x in reversed(k1)], axis=1)
        strided = jnp.concatenate([x.T for x in k2], axis=1)
        even = jnp.concatenate([k2[2], k2[0]], axis=1)
        for h in range(10):
            t1_ref[t, h * 32 : (h + 1) * 32, :] = place(forward, 32 * h, 384).astype(BF16)
            if h % 2 == 0:
                strip = place(even, 32 * h, 384)
            else:
                strip = place(k2[1], 32 * (h + 1), 384)
            t2t_ref[t, h * 32 : (h + 1) * 32, :] = strip.astype(BF16)
        for h in range(8):
            t1t_ref[t, h * 32 : (h + 1) * 32, :] = place(back, 32 * h, 320).astype(BF16)
        for g in range(4):
            t2_ref[t, g * 64 : (g + 1) * 64, :] = place(strided, 64 * g, 320).astype(BF16)


def strip_sum(g, rows, blocks, jump):
    total = None
    for n in range(blocks):
        part = g[n * rows : (n + 1) * rows, n * jump : n * jump + 96]
        total = part if total is None else total + part
    return total


def first_kernel(
    x_ref, og_ref, up_ref, down_ref, bias_ref, t1_ref, t2t_ref, rows_ref,
    grads_ref, gp_ref, act_ref,
    xs_ref, ogs_ref, own_ref,
):
    j = lax.axis_index("sx")
    t = lax.axis_index("sy")
    low = t > 0
    high = t < NY - 1
    none = jnp.zeros((64, 256), BF16)
    for n, cls in enumerate(CLASSES):
        at = slice(n * 256, (n + 1) * 256)
        x = jnp.concatenate(
            [jnp.where(low, up_ref[:, at], none), x_ref[:, at], jnp.where(high, down_ref[:, at], none)],
            axis=0,
        )
        store_variants(xs_ref, x, cls)
    og_main = og_ref[...]
    at = slice(1024, 1280)
    og = jnp.concatenate(
        [jnp.where(low, up_ref[:, at], none), og_main, jnp.where(high, down_ref[:, at], none)], axis=0
    )
    ogs_ref[0] = og
    ogs_ref[1] = ahead(og, 1)
    ogs_ref[2] = ahead(og, 32)
    ogs_ref[3] = ahead(ogs_ref[1], 32)

    row = lax.broadcasted_iota(jnp.int32, (320, 256), 0)
    u = lax.rem(lax.broadcasted_iota(jnp.int32, (320, 256), 1), 32)
    row_ok = ((row >= 32) | low) & ((row < 288) | high)
    bias = bias_ref[...]
    for n, (pd, pw) in enumerate(CLASSES):
        pre = None
        for tap, (a, c) in enumerate(TAPS):
            part = dot(t1_ref[tap], xs_ref[variant(pd, pw, a - 1, c - 1)])
            pre = part if pre is None else pre + part
        pre = pre + bias
        local = 2 * u + pw
        wide = local + (32 * j - 2)
        ok = row_ok & (local >= 1) & (local <= 34) & (wide >= 0) & (wide < W)
        sigma = jax.nn.sigmoid(pre)
        act_ref[n] = jnp.where(ok, pre * sigma, 0.0).astype(BF16)
        grad = None
        for a, sd in ((1, 0),) if pd == 0 else ((2, 0), (0, 1)):
            for c, sw in ((1, 0),) if pw == 0 else ((2, 0), (0, 1)):
                part = dot(t2t_ref[a * 3 + c], ogs_ref[sd * 2 + sw])
                grad = part if grad is None else grad + part
        grad = jnp.where(ok, grad * sigma * (1.0 + pre * (1.0 - sigma)), 0.0)
        gp_ref[n] = grad.astype(BF16)
        mine = (u[32:288] >= 1) & (u[32:288] <= 16)
        own_ref[n] = jnp.where(mine, grad[32:288], 0.0).astype(BF16)

    lane = lax.rem(lax.broadcasted_iota(jnp.int32, (256, 256), 1), 32)
    og_own = jnp.where((lane >= 1) & (lane <= 16), og_main.astype(F32), 0.0).astype(BF16)
    blank = jnp.zeros((64, 32), F32)
    ones_hi = []
    for tap, (a, c) in enumerate(TAPS):
        g = dot_nt(og_own, act_variant(act_ref, a, c))
        two = jnp.concatenate([strip_sum(g, 64, 4, 64), blank], axis=1)
        for s in range(NX):
            grads_ref[s, tap * 8 : (tap + 1) * 8, :] = two[8 * s : 8 * s + 8]
        g = None
        for n, (pd, pw) in enumerate(CLASSES):
            part = dot_nt(own_ref[n], xs_ref[variant(pd, pw, a - 1, c - 1), 32:352, :])
            g = part if g is None else g + part
        ones_hi.append(jnp.concatenate([strip_sum(g, 32, 8, 32), blank[0:32]], axis=1))
    one = jnp.concatenate(ones_hi, axis=0)
    hi = one.astype(BF16)
    rest = one - hi.astype(F32)
    mid = rest.astype(BF16)
    low_part = (rest - mid.astype(F32)).astype(BF16)
    rows = rows_ref[...]
    one = (dot(rows, hi) + dot(rows, mid)) + dot(rows, low_part)
    for s in range(NX):
        grads_ref[s, 72:112, :] = one[s * 40 : (s + 1) * 40]


def act_variant(act_ref, a, c):
    pd, sd = step(0, a - 1)
    pw, sw = step(0, c - 1)
    x = act_ref[pd * 2 + pw]
    if sw:
        x = behind(x, 1)
    if sd:
        x = behind(x, 32)
    return x


def second_kernel(gp_ref, act_ref, t1t_ref, t2_ref, scol_ref, gcol_ref, out_ref, gs_ref):
    out = None
    for tap, (a, c) in enumerate(TAPS):
        part = dot(t2_ref[tap], act_variant(act_ref, a, c))
        out = part if out is None else out + part
    out = dot(out.astype(BF16), scol_ref[...])
    for s in range(NX):
        out_ref[s, 128:160, :] = jnp.concatenate(
            [out[g * 64 + 8 * s : g * 64 + 8 * s + 8] for g in range(4)], axis=0
        ).astype(BF16)
    for n, cls in enumerate(CLASSES):
        store_variants(gs_ref, gp_ref[n], cls)
    grads = []
    for pd, pw in CLASSES:
        vol = None
        for tap, (a, c) in enumerate(TAPS):
            part = dot(t1t_ref[tap], gs_ref[variant(pd, pw, 1 - a, 1 - c)])
            vol = part if vol is None else vol + part
        grads.append(vol.astype(BF16))
    for q in range(2):
        at = slice(q * 128, (q + 1) * 128)
        cat = jnp.concatenate(
            [grads[n][half * 128 : (half + 1) * 128, at] for half in range(2) for n in range(4)], axis=1
        )
        got = move(cat, gcol_ref[...])
        for e in range(4):
            out_ref[4 * q + e, 0:128, :] = got[:, e * 128 : (e + 1) * 128]


def sum_kernel(r_ref, out_ref):
    total = r_ref[0]
    for s in range(1, r_ref.shape[0]):
        total = total + r_ref[s]
    out_ref[...] = total


def append_kernel(g_ref, buf_ref, out_ref):
    one = g_ref[72:112, :]
    hi = one.astype(BF16).astype(F32)
    lo = one - hi
    both = jnp.concatenate([hi, lo], axis=0).astype(BF16)
    for s in range(NX):
        out_ref[s] = both


def last_kernel(
    r_ref, g_ref, fcol_ref, rows_ref, ecol_ref, og_rows_ref, krow_ref,
    strided_ref, two_ref, one_ref, vol_ref, *, out_scale, in_scale,
):
    halves = []
    for q in range(2):
        cat = jnp.concatenate([r_ref[4 * q + s, 0:128, :] for s in range(4)], axis=1)
        halves.append(move(cat, fcol_ref[...]))
    for pd in range(2):
        blocks = []
        for half in range(2):
            at = slice((pd * 2 + half) * 128, (pd * 2 + half + 1) * 128)
            blocks.append(jnp.concatenate([halves[0][:, at], halves[1][:, at]], axis=1))
        vol_ref[pd * 256 : (pd + 1) * 256, :] = move(rows_ref[...], jnp.concatenate(blocks, axis=0))
    cat = jnp.concatenate([r_ref[s, 128:160, :] for s in range(NX)], axis=1)
    got = move(cat, ecol_ref[...])
    got = jnp.concatenate([got[:, e * 128 : (e + 1) * 128] for e in range(8)], axis=0)
    strided_ref[...] = move(og_rows_ref[...], got)
    hi = jnp.concatenate([r_ref[s, 160:200, :].astype(F32) for s in range(NX)], axis=0).astype(BF16)
    lo = jnp.concatenate([r_ref[s, 200:240, :].astype(F32) for s in range(NX)], axis=0).astype(BF16)
    one = (dot(krow_ref[...], hi) + dot(krow_ref[...], lo)) * in_scale
    two = g_ref[0:72, :] * out_scale
    for tap, (a, c) in enumerate(TAPS):
        for b in range(3):
            at = slice(b * 32, (b + 1) * 32)
            one_ref[a * 9 + b * 3 + c] = one[tap * 32 : (tap + 1) * 32, at]
            two_ref[a * 9 + b * 3 + c] = two[tap * 8 : (tap + 1) * 8, at]


def call(body, outs, args, scratch=(), specs=None, out_specs=None, aliases=None, grid=()):
    return pl.pallas_call(
        body,
        out_shape=outs,
        grid=grid,
        in_specs=specs or [pl.BlockSpec(memory_space=pltpu.VMEM)] * len(args),
        out_specs=out_specs or jax.tree.map(lambda _: pl.BlockSpec(memory_space=pltpu.VMEM), outs),
        scratch_shapes=list(scratch),
        input_output_aliases=aliases or {},
        compiler_params=pltpu.CompilerParams(vmem_limit_bytes=VMEM),
    )(*args)


def shape(*dims, dtype=BF16):
    return jax.ShapeDtypeStruct(dims, dtype)


def per_device(volume, kernel_one, bias_one, kernel_two, out_grad):
    out_scale = (8 * 128 * 128) ** (-0.5)
    in_scale = (16 * 256 * 256) ** (-0.5)
    chunks = call(
        pack_kernel,
        shape(NX, 256, 128),
        (
            volume.reshape(512, 256),
            out_grad.reshape(256, 128),
            const(row_order(1, 32, 8)),
            const(row_order(8, 8, 4)),
            const(spread_columns()),
        ),
    )
    got = lax.all_to_all(chunks, "sx", 0, 0)
    t1, t1t, t2, t2t = call(
        weights_kernel,
        (shape(9, 320, 384), shape(9, 256, 320), shape(9, 256, 320), shape(9, 320, 384)),
        (
            kernel_one.transpose(2, 3, 4, 0, 1).reshape(27, C, C),
            kernel_two.transpose(2, 3, 4, 1, 0).reshape(27, C, K),
        ),
    )
    bias = jnp.tile(bias_one.astype(F32), 10)[:, None]
    x, og, up, down = call(
        unpack_kernel,
        (shape(256, 1024), shape(256, 256), shape(64, 1280), shape(64, 1280)),
        (got, const(class_columns()), const(cotangent_columns())),
    )
    up = lax.ppermute(up, "sy", [(i, (i + 1) % NY) for i in range(NY)])
    down = lax.ppermute(down, "sy", [((i + 1) % NY, i) for i in range(NY)])
    grads, gp, act = call(
        first_kernel,
        (shape(NX, 112, 128, dtype=F32), shape(4, 320, 256), shape(4, 320, 256)),
        (x, og, up, down, bias, t1, t2t, const(kernel_rows())),
        scratch=(
            pltpu.VMEM((16, 384, 256), BF16),
            pltpu.VMEM((4, 384, 256), BF16),
            pltpu.VMEM((4, 256, 256), BF16),
        ),
    )
    grads = lax.all_to_all(grads, "sx", 0, 0)
    buffer = call(
        second_kernel,
        shape(NX, 240, 128),
        (gp, act, t1t, t2, const(strided_columns()), const(gather_columns())),
        scratch=(pltpu.VMEM((16, 320, 256), BF16),),
    )
    grads = call(sum_kernel, shape(112, 128, dtype=F32), (grads,))
    for bit in (1, 2, 4, 8, 16):
        grads = grads + lax.ppermute(grads, "sy", [(i, i ^ bit) for i in range(NY)])
    buffer = call(
        append_kernel,
        shape(NX, 240, 128),
        (grads, buffer),
        specs=[pl.BlockSpec((112, 128), lambda n: (0, 0)), pl.BlockSpec(memory_space=pl.ANY)],
        out_specs=pl.BlockSpec((NX, 80, 128), lambda n: (0, 2, 0)),
        grid=(1,),
        aliases={1: 0},
    )
    got = lax.all_to_all(buffer, "sx", 0, 0)
    strided, two, one, vol = call(
        functools.partial(last_kernel, out_scale=out_scale, in_scale=in_scale),
        (shape(256, 128), shape(27, 8, C, dtype=F32), shape(27, C, C, dtype=F32), shape(512, 256)),
        (
            got,
            grads,
            const(plane_columns()),
            const(row_order(1, 8, 32)),
            const(strided_planes()),
            const(row_order(8, 4, 8)),
            const(kernel_rows().T),
        ),
    )
    return (
        strided.reshape(8, 8, 4, 128),
        two.reshape(3, 3, 3, 8, C).transpose(3, 4, 0, 1, 2),
        one.reshape(3, 3, 3, C, C).transpose(3, 4, 0, 1, 2),
        vol.reshape(2, C, 8, W),
    )


def solution(mesh):
    return jax.shard_map(
        per_device,
        mesh=mesh,
        in_specs=(P("sx", None, "sy", None), P(), P(), P(), P(None, "sx", "sy", None)),
        out_specs=(
            P(None, "sx", "sy", None),
            P("sx", None, None, None, None),
            P(),
            P("sx", None, "sy", None),
        ),
        check_vma=False,
    )
```

```python
import functools

import jax
import jax.numpy as jnp
from jax import lax
from jax.experimental import pallas as pl
from jax.experimental.pallas import tpu as pltpu
from jax.sharding import PartitionSpec as P

F32 = jnp.float32
BF16 = jnp.bfloat16
NX = 8
NY = 32
C = 32
K = 64
W = 256
CLASSES = ((0, 0), (0, 1), (1, 0), (1, 1))
TAPS = tuple((a, c) for a in range(3) for c in range(3))


def iota(dims, axis):
    return lax.broadcasted_iota(jnp.int32, dims, axis)


def pick(mask):
    return jnp.where(mask, 1.0, 0.0).astype(BF16)


def dot(a, b):
    return jnp.dot(a, b, preferred_element_type=F32)


def move(a, b):
    return dot(a, b).astype(BF16)


def dot_nt(a, b):
    return lax.dot_general(a, b, (((1,), (1,)), ((), ())), preferred_element_type=F32)


def ahead(x, n):
    return jnp.concatenate([x[:, n:], jnp.zeros((x.shape[0], n), x.dtype)], axis=1)


def behind(x, n):
    return jnp.concatenate([jnp.zeros((x.shape[0], n), x.dtype), x[:, :-n]], axis=1)


def step(parity, offset):
    at = parity + offset
    return (1, 1) if at == -1 else (0, 1) if at == 2 else (at, 0)


def variant(pd, pw, da, dc):
    qd, sd = step(pd, da)
    qw, sw = step(pw, dc)
    return ((qd * 2 + qw) * 2 + sd) * 2 + sw


def variants(x, cls):
    move_d = behind if cls[0] else ahead
    move_w = behind if cls[1] else ahead
    along = move_w(x, 1)
    return x, along, move_d(x, 32), move_d(along, 32)


def store_variants(ref, x, cls):
    base = (cls[0] * 2 + cls[1]) * 4
    for n, form in enumerate(variants(x, cls)):
        ref[base + n] = form


def pack_kernel(vol_hbm, og_hbm, out_ref, vol_ref, og_ref, sems):
    copies = (
        pltpu.make_async_copy(vol_hbm, vol_ref, sems.at[0]),
        pltpu.make_async_copy(og_hbm, og_ref, sems.at[1]),
    )
    for copy in copies:
        copy.start()
    row = iota((256, 256), 0)
    col = iota((256, 256), 1)
    by_row = pick(col == (row & 31) * 8 + (row >> 5))
    by_kind = pick(col == (row & ~31) + (row & 7) * 4 + ((row >> 3) & 3))
    lane = iota((1, 128), 1)
    cls = jnp.where(lane >= 20, 1, 0) + jnp.where(lane >= 40, 1, 0) + jnp.where(lane >= 60, 1, 0)
    u = lane - 20 * cls
    at = iota((128, 128), 0)
    chosen = []
    for j in range(NX):
        w = jnp.where((lane < 80) & (u < 18), 32 * j - 2 + 2 * u + (cls & 1), -1)
        pieces = []
        for pd in range(2):
            from_plane = jnp.where(cls >> 1 == pd, w, -1)
            for block in range(max(0, 32 * j - 2) // 128, min(W - 1, 32 * j + 33) // 128 + 1):
                pieces.append((pd, block, pick(at + 128 * block == from_plane)))
        g = jnp.where((lane >= 80) & (lane < 98), 16 * j - 1 + lane - 80, -1)
        pieces.append((2, 0, pick(at == g)))
        chosen.append(pieces)
    for copy in copies:
        copy.wait()
    planes = (
        move(by_row, vol_ref[0:256]),
        move(by_row, vol_ref[256:512]),
        move(by_kind, og_ref[...]),
    )
    for j in range(NX):
        cat = jnp.concatenate(
            [planes[n][:, block * 128 : (block + 1) * 128] for n, block, _ in chosen[j]], axis=1
        )
        out_ref[j] = move(cat, jnp.concatenate([m for _, _, m in chosen[j]], axis=0))


def unpack_kernel(r_ref, cls_ref, og_cols_ref, x_ref, og_ref, up_ref, down_ref):
    for q in range(2):
        cat = jnp.concatenate([r_ref[4 * q + s] for s in range(4)], axis=1)
        got = move(cat, cls_ref[...])
        for cls in range(4):
            at = slice(cls * 256 + q * 128, cls * 256 + (q + 1) * 128)
            part = got[:, cls * 128 : (cls + 1) * 128]
            x_ref[:, at] = part
            up_ref[:, at] = part[192:256]
            down_ref[:, at] = part[0:64]
    parts = []
    for s in range(NX):
        parts.append(jnp.concatenate([r_ref[s, e * 32 : (e + 1) * 32, :] for e in range(8)], axis=1))
    og = dot(jnp.concatenate(parts, axis=0), og_cols_ref[...])
    og = jnp.concatenate(
        [og[s * 32 + g * 8 : s * 32 + g * 8 + 8] for g in range(4) for s in range(NX)], axis=0
    ).astype(BF16)
    og_ref[...] = og
    up_ref[:, 1024:1280] = og[192:256]
    down_ref[:, 1024:1280] = og[0:64]


def place(strip, offset, width):
    if offset >= width:
        return jnp.zeros((strip.shape[0], width), strip.dtype)
    first = max(0, -offset)
    strip = strip[:, first : min(strip.shape[1], width - offset)]
    offset += first
    parts = [strip]
    if offset:
        parts.insert(0, jnp.zeros((strip.shape[0], offset), strip.dtype))
    rest = width - offset - strip.shape[1]
    if rest:
        parts.append(jnp.zeros((strip.shape[0], rest), strip.dtype))
    return jnp.concatenate(parts, axis=1)


def from_row(rows, target):
    return pick(iota((rows, target.shape[1]), 0) == target)


def kernel_blocks(ref, a, c):
    return [ref[a * 9 + b * 3 + c].astype(F32) for b in range(3)]


def weights_kernel(
    k1_ref, k2_ref, strips_ref, even_ref, odd_ref, t1h_ref, t2th_ref, cls_ref, og_cols_ref
):
    col = iota((1, 512), 1)
    u = col & 31
    cls_ref[...] = from_row(512, jnp.where(u < 18, ((col >> 5) & 3) * 128 + (col >> 7) * 20 + u, -1))
    col, u = col[:, 0:256], u[:, 0:256]
    og_cols_ref[...] = from_row(1024, jnp.where(u < 18, (col >> 5) * 128 + 80 + u, -1))
    gap = jnp.zeros((C, C), F32)
    wide = jnp.zeros((C, K), F32)
    for t, (a, c) in enumerate(TAPS):
        k1 = kernel_blocks(k1_ref, a, c)
        k2 = kernel_blocks(k2_ref, a, c)
        forward = jnp.concatenate(k1, axis=1)
        even = jnp.concatenate([k2[2], k2[0]], axis=1)
        for r in range(4):
            strips_ref[t, r] = place(forward, 32 * r, 256).astype(BF16)
        for r in range(2):
            even_ref[t, r] = place(even, 64 * r, 256).astype(BF16)
            odd_ref[t, r] = place(k2[1], 64 * r, 128).astype(BF16)
        rim = (
            (k1[0], k1[1], gap, gap),
            (gap, k1[0], gap, gap),
            (gap, gap, k1[2], gap),
            (gap, gap, k1[1], k1[2]),
        )
        t1h_ref[:, t * 128 : (t + 1) * 128] = jnp.concatenate(
            [jnp.concatenate(r, axis=1) for r in rim], axis=0
        ).astype(BF16)
        rim = ((k2[2], wide), (wide, wide), (wide, k2[0]), (wide, k2[1]))
        t2th_ref[t] = jnp.concatenate([jnp.concatenate(r, axis=1) for r in rim], axis=0).astype(BF16)


def window(strip, at):
    if at == 0:
        return strip
    none = jnp.zeros((strip.shape[0], 128), strip.dtype)
    return jnp.concatenate([strip[:, 128:], none] if at < 0 else [none, strip[:, :128]], axis=1)


def build_forward(strips_ref, even_ref, odd_ref, t1_ref, t2t_ref):
    none = jnp.zeros((C, 128), BF16)
    for t in range(9):
        for h in range(10):
            at = slice(h * 32, (h + 1) * 32)
            r = (h + 2) % 4
            t1_ref[t, at, :] = window(strips_ref[t, r], (h - 2 - r) // 4)
            if h % 2 == 0:
                r = (h // 2 + 1) % 2
                t2t_ref[t, at, :] = window(even_ref[t, r], (h // 2 - 1 - r) // 2)
            else:
                n = h // 2
                strip = odd_ref[t, n % 2] if n < 4 else none
                t2t_ref[t, at, :] = jnp.concatenate([none, strip] if n > 1 else [strip, none], axis=1)


def build_back(k1_ref, k2_ref, t1t_ref, t2_ref):
    for t, (a, c) in enumerate(TAPS):
        back = jnp.concatenate([x.T for x in reversed(kernel_blocks(k1_ref, a, c))], axis=1)
        strided = jnp.concatenate([x.T for x in kernel_blocks(k2_ref, a, c)], axis=1)
        for h in range(8):
            t1t_ref[t, h * 32 : (h + 1) * 32, :] = place(back, 32 * h, 320).astype(BF16)
        for g in range(4):
            t2_ref[t, g * 64 : (g + 1) * 64, :] = place(strided, 64 * g, 320).astype(BF16)


def strip_sum(g, blocks, jump):
    width = g.shape[1] // blocks
    total = None
    for n in range(blocks):
        part = g[n * jump : n * jump + 96, n * width : (n + 1) * width]
        total = part if total is None else total + part
    return total


def conv_taps(pd, pw, sign):
    return [(tap, variant(pd, pw, sign * (a - 1), sign * (c - 1))) for tap, (a, c) in enumerate(TAPS)]


def spread_taps(pd, pw):
    depth = ((1, 0),) if pd == 0 else ((2, 0), (0, 1))
    width = ((1, 0),) if pw == 0 else ((2, 0), (0, 1))
    return [(a * 3 + c, sd * 2 + sw) for a, sd in depth for c, sw in width]


def tap_sum(weights_ref, inputs_ref, pairs):
    total = None
    for tap, at in pairs:
        part = dot(weights_ref[tap], inputs_ref[at])
        total = part if total is None else total + part
    return total


def store_cotangents(ref, og):
    along = ahead(og, 1)
    ref[0] = og
    ref[1] = along
    ref[2] = ahead(og, 32)
    ref[3] = ahead(along, 32)


def inner_kernel(
    x_ref, og_ref, strips_ref, even_ref, odd_ref,
    xs_ref, pre_ref, grad_ref,
    ogs_ref, t1_ref, t2t_ref,
):
    build_forward(strips_ref, even_ref, odd_ref, t1_ref, t2t_ref)
    for n, cls in enumerate(CLASSES):
        store_variants(xs_ref, x_ref[:, n * 256 : (n + 1) * 256], cls)
    store_cotangents(ogs_ref, og_ref[...])
    for n, (pd, pw) in enumerate(CLASSES):
        pre_ref[n] = tap_sum(t1_ref, xs_ref, conv_taps(pd, pw, 1))
        grad_ref[n] = tap_sum(t2t_ref, ogs_ref, spread_taps(pd, pw))


def first_kernel(
    xs_ref, pre_ref, ga_ref, og_ref, up_ref, down_ref, bias_ref, t1h_ref, t2th_ref,
    grads_ref, gp_ref, act_ref,
    rim_ref, ogs_ref, own_ref,
):
    j = lax.axis_index("sx")
    t = lax.axis_index("sy")
    low = t > 0
    high = t < NY - 1
    none = jnp.zeros((64, 256), BF16)

    def rim(at):
        return jnp.concatenate(
            [jnp.where(low, up_ref[:, at], none), jnp.where(high, down_ref[:, at], none)], axis=0
        )

    uses = [
        (n, tap, at) for n, (pd, pw) in enumerate(CLASSES) for tap, at in conv_taps(pd, pw, 1)
    ]
    for n, cls in enumerate(CLASSES):
        forms = variants(rim(slice(n * 256, (n + 1) * 256)), cls)
        for m, tap, at in uses:
            if at // 4 == n:
                rim_ref[m, tap * 128 : (tap + 1) * 128, :] = forms[at % 4]
    store_cotangents(ogs_ref, rim(slice(1024, 1280)))

    def with_rim(inner, outer):
        return jnp.concatenate(
            [inner[0:64] + outer[0:64], inner[64:256], inner[256:320] + outer[64:128]], axis=0
        )

    row = lax.broadcasted_iota(jnp.int32, (320, 256), 0)
    u = lax.rem(lax.broadcasted_iota(jnp.int32, (320, 256), 1), 32)
    row_ok = ((row >= 32) | low) & ((row < 288) | high)
    bias = bias_ref[...]
    for n, (pd, pw) in enumerate(CLASSES):
        pre = with_rim(pre_ref[n], dot(t1h_ref[...], rim_ref[n])) + bias
        local = 2 * u + pw
        wide = local + (32 * j - 2)
        ok = row_ok & (local >= 1) & (local <= 34) & (wide >= 0) & (wide < W)
        sigma = jax.nn.sigmoid(pre)
        act_ref[n] = jnp.where(ok, pre * sigma, 0.0).astype(BF16)
        grad = with_rim(ga_ref[n], tap_sum(t2th_ref, ogs_ref, spread_taps(pd, pw)))
        grad = jnp.where(ok, grad * sigma * (1.0 + pre * (1.0 - sigma)), 0.0)
        gp_ref[n] = grad.astype(BF16)
        mine = (u[32:288] >= 1) & (u[32:288] <= 16)
        own_ref[n] = jnp.where(mine, grad[32:288], 0.0).astype(BF16)

    lane = lax.rem(lax.broadcasted_iota(jnp.int32, (256, 256), 1), 32)
    og_own = jnp.where((lane >= 1) & (lane <= 16), og_ref[...].astype(F32), 0.0).astype(BF16)
    twos, ones = [], []
    for tap, (a, c) in enumerate(TAPS):
        twos.append(strip_sum(dot_nt(act_variant(act_ref, a, c), og_own), 4, 64))
        g = None
        for n, (pd, pw) in enumerate(CLASSES):
            at = variant(pd, pw, a - 1, c - 1)
            first = tap * 128 + 32
            x = jnp.concatenate(
                [
                    rim_ref[n, first : first + 32, :],
                    xs_ref[at],
                    rim_ref[n, first + 32 : first + 64, :],
                ],
                axis=0,
            )
            part = dot_nt(x, own_ref[n])
            g = part if g is None else g + part
        ones.append(strip_sum(g, 8, 32))
    twos.append(jnp.zeros((32, K), F32))
    ones.append(jnp.zeros((32, C), F32))
    twos = jnp.concatenate(twos, axis=0)
    ones = jnp.concatenate(ones, axis=0)
    twos = [twos[n * 128 : (n + 1) * 128].T for n in range(7)]
    ones = [ones[n * 128 : (n + 1) * 128].T for n in range(7)] + [jnp.zeros((C, 128), F32)] * 3
    for s in range(NX):
        for n in range(12):
            if n < 7:
                tile = twos[n][8 * s : 8 * s + 8]
            else:
                pair = ones[2 * n - 14], ones[2 * n - 13]
                tile = jnp.concatenate([x[4 * s : 4 * s + 4] for x in pair], axis=0)
            grads_ref[s * 2 + n // 6, n % 6 * 8 : n % 6 * 8 + 8, :] = tile


def act_variant(act_ref, a, c):
    pd, sd = step(0, a - 1)
    pw, sw = step(0, c - 1)
    x = act_ref[pd * 2 + pw]
    if sw:
        x = behind(x, 1)
    if sd:
        x = behind(x, 32)
    return x


def second_kernel(
    gp_ref, act_ref, k1_ref, k2_ref,
    out_ref, fcol_ref, rows_ref, og_rows_ref,
    gs_ref, t1t_ref, t2_ref,
):
    col = iota((1, 512), 1)
    half = (col >> 6) & 1
    gather_cols = from_row(
        1024, half * 512 + ((col >> 4) & 3) * 128 + (col >> 7) * 32 + 1 + (col & 15)
    )
    fcol_ref[...] = from_row(
        512,
        ((col >> 5) & 3) * 128
        + ((col >> 7) & 1) * 64
        + ((col >> 8) * 2 + (col & 1)) * 16
        + ((col & 31) >> 1),
    )
    col = col[:, 0:128]
    strided_cols = from_row(256, (col >> 4) * 32 + 1 + (col & 15))
    row = iota((256, 256), 0)
    col = iota((256, 256), 1)
    rows_ref[...] = pick(col == (row & 7) * 32 + (row >> 3))
    og_rows_ref[...] = pick(col == (row & ~31) + (row & 3) * 8 + ((row >> 2) & 7))
    build_back(k1_ref, k2_ref, t1t_ref, t2_ref)
    out = None
    for tap, (a, c) in enumerate(TAPS):
        part = dot(t2_ref[tap], act_variant(act_ref, a, c))
        out = part if out is None else out + part
    out = dot(out.astype(BF16), strided_cols)
    for s in range(NX):
        out_ref[s, 128:160, :] = jnp.concatenate(
            [out[g * 64 + 8 * s : g * 64 + 8 * s + 8] for g in range(4)], axis=0
        ).astype(BF16)
    for n, cls in enumerate(CLASSES):
        store_variants(gs_ref, gp_ref[n], cls)
    grads = [tap_sum(t1t_ref, gs_ref, conv_taps(pd, pw, -1)).astype(BF16) for pd, pw in CLASSES]
    for q in range(2):
        at = slice(q * 128, (q + 1) * 128)
        cat = jnp.concatenate(
            [grads[n][half * 128 : (half + 1) * 128, at] for half in range(2) for n in range(4)], axis=1
        )
        got = move(cat, gather_cols)
        for e in range(4):
            out_ref[4 * q + e, 0:128, :] = got[:, e * 128 : (e + 1) * 128]


def sum_kernel(r_ref, after_ref, out_ref):
    total = r_ref[0]
    for s in range(1, r_ref.shape[0]):
        total = total + r_ref[s]
    out_ref[...] = total


def pair_kernel(a_ref, b_ref, out_ref):
    total = a_ref[...] + b_ref[...]
    for n in range(out_ref.shape[0]):
        out_ref[n] = total


def append_kernel(mine_ref, other_ref, buf_ref, out_ref, two_ref):
    first = lax.rem(lax.axis_index("sy"), 2) == 0
    mine, other = mine_ref[...], other_ref[...]
    even = jnp.where(first, mine, other)
    odd = jnp.where(first, other, mine)
    total = jnp.concatenate([even, odd], axis=0)
    two_ref[...] = total[0:56]
    one = total[56:96]
    hi = one.astype(BF16).astype(F32)
    both = jnp.concatenate([hi, one - hi], axis=0).astype(BF16)
    for s in range(NX):
        out_ref[s] = both


def last_kernel(
    r_ref, g_ref, fcol_ref, rows_ref, og_rows_ref,
    strided_ref, two_ref, one_ref, vol_ref, *, out_scale, in_scale,
):
    halves = []
    for q in range(2):
        cat = jnp.concatenate([r_ref[4 * q + s, 0:128, :] for s in range(4)], axis=1)
        halves.append(move(cat, fcol_ref[...]))
    for pd in range(2):
        blocks = []
        for half in range(2):
            at = slice((pd * 2 + half) * 128, (pd * 2 + half + 1) * 128)
            blocks.append(jnp.concatenate([halves[0][:, at], halves[1][:, at]], axis=1))
        vol_ref[pd * 256 : (pd + 1) * 256, :] = move(rows_ref[...], jnp.concatenate(blocks, axis=0))
    parts = [r_ref[s, 128:160, :].astype(F32) for s in range(NX)]
    group = iota((32, 128), 1) >> 4
    blocks = []
    for e in range(8):
        block = None
        for j in range(NX):
            turned = pltpu.roll(parts[j], (j - e) * 16 % 128, 1) if j != e else parts[j]
            block = turned if block is None else jnp.where(group == j, turned, block)
        blocks.append(block)
    strided_ref[...] = move(og_rows_ref[...], jnp.concatenate(blocks, axis=0).astype(BF16))
    sums = [r_ref[s, 160:200, :].astype(F32) + r_ref[s, 200:240, :].astype(F32) for s in range(NX)]
    two = g_ref[...] * out_scale
    for n in range(7):
        one = jnp.concatenate([x[4 * n : 4 * n + 4] for x in sums], axis=0) * in_scale
        for m in range(4 * n, min(4 * n + 4, 27)):
            a, c = TAPS[m // 3]
            tap = a * 9 + m % 3 * 3 + c
            at = slice((m - 4 * n) * 32, (m - 4 * n + 1) * 32)
            one_ref[tap] = one[:, at]
            two_ref[tap] = two[n * 8 : (n + 1) * 8, at]


def call(body, outs, args, scratch=(), specs=None, out_specs=None, aliases=None, grid=(), us=1, vmem=16):
    return pl.pallas_call(
        body,
        out_shape=outs,
        grid=grid,
        in_specs=specs or [pl.BlockSpec(memory_space=pltpu.VMEM)] * len(args),
        out_specs=out_specs or jax.tree.map(lambda _: pl.BlockSpec(memory_space=pltpu.VMEM), outs),
        scratch_shapes=list(scratch),
        input_output_aliases=aliases or {},
        compiler_params=pltpu.CompilerParams(vmem_limit_bytes=vmem * 1024 * 1024),
        cost_estimate=pl.CostEstimate(flops=us * 10**9, bytes_accessed=0, transcendentals=0),
    )(*args)


def whole(*dims):
    return pl.BlockSpec(dims, lambda n: (0,) * len(dims))


def shape(*dims, dtype=BF16):
    return jax.ShapeDtypeStruct(dims, dtype)


def per_device(volume, kernel_one, bias_one, kernel_two, out_grad):
    out_scale = (8 * 128 * 128) ** (-0.5)
    in_scale = (16 * 256 * 256) ** (-0.5)
    chunks = call(
        pack_kernel,
        shape(NX, 256, 128),
        (volume.reshape(512, 256), out_grad.reshape(256, 128)),
        specs=[pl.BlockSpec(memory_space=pl.ANY)] * 2,
        scratch=(
            pltpu.VMEM((512, 256), BF16),
            pltpu.VMEM((256, 128), BF16),
            pltpu.SemaphoreType.DMA((2,)),
        ),
        vmem=60,
    )
    got = lax.all_to_all(chunks, "sx", 0, 0)
    k1 = kernel_one.transpose(2, 3, 4, 0, 1).reshape(27, C, C)
    k2 = kernel_two.transpose(2, 3, 4, 1, 0).reshape(27, C, K)
    strips, even, odd, t1h, t2th, class_cols, og_cols = call(
        weights_kernel,
        (
            shape(9, 4, 32, 256), shape(9, 2, 32, 256), shape(9, 2, 32, 128),
            shape(128, 9 * 128), shape(9, 128, 128), shape(512, 512), shape(1024, 256),
        ),
        (k1, k2),
        us=3,
    )
    bias = jnp.tile(bias_one.astype(F32), 10)[:, None]
    x, og, up, down = call(
        unpack_kernel,
        (shape(256, 1024), shape(256, 256), shape(64, 1280), shape(64, 1280)),
        (got, class_cols, og_cols),
    )
    up = lax.ppermute(up, "sy", [(i, (i + 1) % NY) for i in range(NY)])
    down = lax.ppermute(down, "sy", [((i + 1) % NY, i) for i in range(NY)])
    xs, pre, grad_act = call(
        inner_kernel,
        (shape(16, 256, 256), shape(4, 320, 256, dtype=F32), shape(4, 320, 256, dtype=F32)),
        (x, og, strips, even, odd),
        scratch=(
            pltpu.VMEM((4, 256, 256), BF16),
            pltpu.VMEM((9, 320, 256), BF16),
            pltpu.VMEM((9, 320, 256), BF16),
        ),
        us=5,
    )
    grads, gp, act = call(
        first_kernel,
        (shape(2 * NX, 48, 128, dtype=F32), shape(4, 320, 256), shape(4, 320, 256)),
        (xs, pre, grad_act, og, up, down, bias, t1h, t2th),
        scratch=(
            pltpu.VMEM((4, 9 * 128, 256), BF16),
            pltpu.VMEM((4, 128, 256), BF16),
            pltpu.VMEM((4, 256, 256), BF16),
        ),
        us=5,
    )
    grads = lax.all_to_all(
        grads,
        ("sx", "sy"),
        0,
        0,
        axis_index_groups=[
            [s * NY + 2 * q + r for s in range(NX) for r in range(2)] for q in range(NY // 2)
        ],
    )
    buffer, plane_cols, rows_back, og_rows_back = call(
        second_kernel,
        (shape(NX, 240, 128), shape(512, 512), shape(256, 256), shape(256, 256)),
        (gp, act, k1, k2),
        scratch=(
            pltpu.VMEM((16, 320, 256), BF16),
            pltpu.VMEM((9, 256, 320), BF16),
            pltpu.VMEM((9, 256, 320), BF16),
        ),
        us=6,
        vmem=20,
    )
    both = [pl.BlockSpec(memory_space=pltpu.VMEM), pl.BlockSpec(memory_space=pl.ANY)]
    keep = call(sum_kernel, shape(48, 128, dtype=F32), (grads, buffer), specs=both)
    keep = call(
        pair_kernel,
        shape(8, 48, 128, dtype=F32),
        (keep, lax.ppermute(keep, "sy", [(i, i ^ 2) for i in range(NY)])),
    )
    keep = lax.all_to_all(
        keep, "sy", 0, 0, axis_index_groups=[list(range(r, NY, 4)) for r in range(4)]
    )
    keep = call(sum_kernel, shape(48, 128, dtype=F32), (keep, buffer), specs=both)
    other = lax.ppermute(keep, "sy", [(i, i ^ 1) for i in range(NY)])
    buffer, two = call(
        append_kernel,
        (shape(NX, 240, 128), shape(56, 128, dtype=F32)),
        (keep, other, buffer),
        specs=[whole(48, 128), whole(48, 128), pl.BlockSpec(memory_space=pl.ANY)],
        out_specs=(pl.BlockSpec((NX, 80, 128), lambda n: (0, 2, 0)), whole(56, 128)),
        grid=(1,),
        aliases={2: 0},
    )
    got = lax.all_to_all(buffer, "sx", 0, 0)
    strided, two, one, vol = call(
        functools.partial(last_kernel, out_scale=out_scale, in_scale=in_scale),
        (shape(256, 128), shape(27, 8, C, dtype=F32), shape(27, C, C, dtype=F32), shape(512, 256)),
        (got, two, plane_cols, rows_back, og_rows_back),
    )
    return (
        strided.reshape(8, 8, 4, 128),
        two.reshape(3, 3, 3, 8, C).transpose(3, 4, 0, 1, 2),
        one.reshape(3, 3, 3, C, C).transpose(3, 4, 0, 1, 2),
        vol.reshape(2, C, 8, W),
    )


def solution(mesh):
    return jax.shard_map(
        per_device,
        mesh=mesh,
        in_specs=(P("sx", None, "sy", None), P(), P(), P(), P(None, "sx", "sy", None)),
        out_specs=(
            P(None, "sx", "sy", None),
            P("sx", None, None, None, None),
            P(),
            P("sx", None, "sy", None),
        ),
        check_vma=False,
    )
```

```python
import functools

import jax
import jax.numpy as jnp
from jax import lax
from jax.experimental import pallas as pl
from jax.experimental.pallas import tpu as pltpu
from jax.sharding import PartitionSpec as P

F32 = jnp.float32
BF16 = jnp.bfloat16
NX = 8
NY = 32
C = 32
K = 64
W = 256
CLASSES = ((0, 0), (0, 1), (1, 0), (1, 1))
TAPS = tuple((a, c) for a in range(3) for c in range(3))


def iota(dims, axis):
    return lax.broadcasted_iota(jnp.int32, dims, axis)


def pick(mask):
    return jnp.where(mask, 1.0, 0.0).astype(BF16)


def dot(a, b):
    return jnp.dot(a, b, preferred_element_type=F32)


def move(a, b):
    return dot(a, b).astype(BF16)


def dot_nt(a, b):
    return lax.dot_general(a, b, (((1,), (1,)), ((), ())), preferred_element_type=F32)


def ahead(x, n):
    return jnp.concatenate([x[:, n:], jnp.zeros((x.shape[0], n), x.dtype)], axis=1)


def behind(x, n):
    return jnp.concatenate([jnp.zeros((x.shape[0], n), x.dtype), x[:, :-n]], axis=1)


def step(parity, offset):
    at = parity + offset
    return (1, 1) if at == -1 else (0, 1) if at == 2 else (at, 0)


def variant(pd, pw, da, dc):
    qd, sd = step(pd, da)
    qw, sw = step(pw, dc)
    return ((qd * 2 + qw) * 2 + sd) * 2 + sw


def variants(x, cls):
    move_d = behind if cls[0] else ahead
    move_w = behind if cls[1] else ahead
    along = move_w(x, 1)
    return x, along, move_d(x, 32), move_d(along, 32)


def store_variants(ref, x, cls):
    base = (cls[0] * 2 + cls[1]) * 4
    for n, form in enumerate(variants(x, cls)):
        ref[base + n] = form


def pack_kernel(vol_hbm, og_hbm, out_hbm, vol_ref, og_ref, out_ref, sems):
    copies = (
        pltpu.make_async_copy(vol_hbm, vol_ref, sems.at[0]),
        pltpu.make_async_copy(og_hbm, og_ref, sems.at[1]),
    )
    for copy in copies:
        copy.start()
    row = iota((256, 256), 0)
    col = iota((256, 256), 1)
    by_row = pick(col == (row & 31) * 8 + (row >> 5))
    by_kind = pick(col == ((row >> 3) & 7) * 32 + (row & 7) * 4 + (row >> 6))
    lane = iota((1, 128), 1)
    cls = jnp.where(lane >= 20, 1, 0) + jnp.where(lane >= 40, 1, 0) + jnp.where(lane >= 60, 1, 0)
    u = lane - 20 * cls
    at = iota((128, 128), 0)
    chosen = []
    for j in range(NX):
        w = jnp.where((lane < 80) & (u < 18), 32 * j - 2 + 2 * u + (cls & 1), -1)
        pieces = []
        for pd in range(2):
            from_plane = jnp.where(cls >> 1 == pd, w, -1)
            for block in range(max(0, 32 * j - 2) // 128, min(W - 1, 32 * j + 33) // 128 + 1):
                pieces.append((pd, block, pick(at + 128 * block == from_plane)))
        g = jnp.where((lane >= 80) & (lane < 98), 16 * j - 1 + lane - 80, -1)
        pieces.append((2, 0, pick(at == g)))
        chosen.append(pieces)
    for copy in copies:
        copy.wait()
    planes = (
        move(by_row, vol_ref[0:256]),
        move(by_row, vol_ref[256:512]),
        move(by_kind, og_ref[...]),
    )
    for j in range(NX):
        cat = jnp.concatenate(
            [planes[n][:, block * 128 : (block + 1) * 128] for n, block, _ in chosen[j]], axis=1
        )
        out_ref[j] = move(cat, jnp.concatenate([m for _, _, m in chosen[j]], axis=0))
        copies += (pltpu.make_async_copy(out_ref.at[j], out_hbm.at[j], sems.at[2 + j]),)
        copies[-1].start()
    for copy in copies[2:]:
        copy.wait()


def split_kernel(r_ref, cross_ref, pair_ref):
    even = lax.rem(lax.axis_index("sy"), 2) == 0
    for s in range(NX):
        top, bottom = r_ref[s, 0:64, :], r_ref[s, 192:256, :]
        cross_ref[s] = jnp.where(even, top, bottom)
        pair_ref[s] = jnp.where(even, bottom, top)


def by_class(parts, cls_cols):
    got = [move(jnp.concatenate(parts[4 * q : 4 * q + 4], axis=1), cls_cols) for q in range(2)]
    return [
        jnp.concatenate([x[:, n * 128 : (n + 1) * 128] for x in got], axis=1) for n in range(4)
    ]


def cotangents(parts, groups, og_cols):
    parts = [x.astype(F32) for x in parts]
    cat = [
        jnp.concatenate(
            [x[g * 64 + e * 8 : g * 64 + e * 8 + 8] for g in range(groups) for x in parts], axis=0
        )
        for e in range(8)
    ]
    return move(jnp.concatenate(cat, axis=1).astype(BF16), og_cols)


def place(strip, offset, width):
    if offset >= width:
        return jnp.zeros((strip.shape[0], width), strip.dtype)
    first = max(0, -offset)
    strip = strip[:, first : min(strip.shape[1], width - offset)]
    offset += first
    parts = [strip]
    if offset:
        parts.insert(0, jnp.zeros((strip.shape[0], offset), strip.dtype))
    rest = width - offset - strip.shape[1]
    if rest:
        parts.append(jnp.zeros((strip.shape[0], rest), strip.dtype))
    return jnp.concatenate(parts, axis=1)


def from_row(rows, target):
    return pick(iota((rows, target.shape[1]), 0) == target)


def kernel_blocks(ref, a, c):
    return [ref[a * 9 + b * 3 + c].astype(F32) for b in range(3)]


def weights_kernel(
    k1_ref, k2_ref, strips_ref, even_ref, odd_ref, cls_ref, og_cols_ref
):
    col = iota((1, 512), 1)
    u = col & 31
    cls_ref[...] = from_row(512, jnp.where(u < 18, ((col >> 5) & 3) * 128 + (col >> 7) * 20 + u, -1))
    col, u = col[:, 0:256], u[:, 0:256]
    og_cols_ref[...] = from_row(1024, jnp.where(u < 18, (col >> 5) * 128 + 80 + u, -1))
    for t, (a, c) in enumerate(TAPS):
        k1 = kernel_blocks(k1_ref, a, c)
        k2 = kernel_blocks(k2_ref, a, c)
        forward = jnp.concatenate(k1, axis=1)
        even = jnp.concatenate([k2[2], k2[0]], axis=1)
        for r in range(4):
            strips_ref[t, r] = place(forward, 32 * r, 256).astype(BF16)
        for r in range(2):
            even_ref[t, r] = place(even, 64 * r, 256).astype(BF16)
            odd_ref[t, r] = place(k2[1], 64 * r, 128).astype(BF16)


def rim_kernel(k1_ref, k2_ref, t1h_ref, t2th_ref):
    gap = jnp.zeros((C, C), F32)
    wide = jnp.zeros((C, K), F32)
    for t, (a, c) in enumerate(TAPS):
        k1 = kernel_blocks(k1_ref, a, c)
        k2 = kernel_blocks(k2_ref, a, c)
        rim = (
            (k1[0], k1[1], gap, gap),
            (gap, k1[0], gap, gap),
            (gap, gap, k1[2], gap),
            (gap, gap, k1[1], k1[2]),
        )
        t1h_ref[:, t * 128 : (t + 1) * 128] = jnp.concatenate(
            [jnp.concatenate(r, axis=1) for r in rim], axis=0
        ).astype(BF16)
        rim = ((k2[2], wide), (wide, wide), (wide, k2[0]), (wide, k2[1]))
        t2th_ref[t] = jnp.concatenate([jnp.concatenate(r, axis=1) for r in rim], axis=0).astype(BF16)


def window(strip, at):
    if at == 0:
        return strip
    none = jnp.zeros((strip.shape[0], 128), strip.dtype)
    return jnp.concatenate([strip[:, 128:], none] if at < 0 else [none, strip[:, :128]], axis=1)


def build_forward(strips_ref, even_ref, odd_ref, t1_ref, t2t_ref):
    none = jnp.zeros((C, 128), BF16)
    for t in range(9):
        for h in range(10):
            at = slice(h * 32, (h + 1) * 32)
            r = (h + 2) % 4
            t1_ref[t, at, :] = window(strips_ref[t, r], (h - 2 - r) // 4)
            if h % 2 == 0:
                r = (h // 2 + 1) % 2
                t2t_ref[t, at, :] = window(even_ref[t, r], (h // 2 - 1 - r) // 2)
            else:
                n = h // 2
                strip = odd_ref[t, n % 2] if n < 4 else none
                t2t_ref[t, at, :] = jnp.concatenate([none, strip] if n > 1 else [strip, none], axis=1)


def build_back(k1_ref, k2_ref, t1t_ref, t2_ref):
    for t, (a, c) in enumerate(TAPS):
        back = jnp.concatenate([x.T for x in reversed(kernel_blocks(k1_ref, a, c))], axis=1)
        strided = jnp.concatenate([x.T for x in kernel_blocks(k2_ref, a, c)], axis=1)
        for h in range(8):
            t1t_ref[t, h * 32 : (h + 1) * 32, :] = place(back, 32 * h, 320).astype(BF16)
        for g in range(4):
            t2_ref[t, g * 64 : (g + 1) * 64, :] = place(strided, 64 * g, 320).astype(BF16)


def strip_sum(g, blocks, jump):
    width = g.shape[1] // blocks
    total = None
    for n in range(blocks):
        part = g[n * jump : n * jump + 96, n * width : (n + 1) * width]
        total = part if total is None else total + part
    return total


def conv_taps(pd, pw, sign):
    return [(tap, variant(pd, pw, sign * (a - 1), sign * (c - 1))) for tap, (a, c) in enumerate(TAPS)]


def spread_taps(pd, pw):
    depth = ((1, 0),) if pd == 0 else ((2, 0), (0, 1))
    width = ((1, 0),) if pw == 0 else ((2, 0), (0, 1))
    return [(a * 3 + c, sd * 2 + sw) for a, sd in depth for c, sw in width]


def tap_sum(weights_ref, inputs_ref, pairs):
    total = None
    for tap, at in pairs:
        part = dot(weights_ref[tap], inputs_ref[at])
        total = part if total is None else total + part
    return total


def store_cotangents(ref, og):
    along = ahead(og, 1)
    ref[0] = og
    ref[1] = along
    ref[2] = ahead(og, 32)
    ref[3] = ahead(along, 32)


def inner_kernel(
    r_ref, cls_ref, og_cols_ref, strips_ref, even_ref, odd_ref,
    og_ref, xs_ref, pre_ref, grad_ref,
    ogs_ref, t1_ref, t2t_ref,
):
    build_forward(strips_ref, even_ref, odd_ref, t1_ref, t2t_ref)
    parts = [r_ref[s] for s in range(NX)]
    for x, cls in zip(by_class(parts, cls_ref[...]), CLASSES):
        store_variants(xs_ref, x, cls)
    og_ref[...] = cotangents(parts, 4, og_cols_ref[...])
    store_cotangents(ogs_ref, og_ref[...])
    for n, (pd, pw) in enumerate(CLASSES):
        pre_ref[n] = tap_sum(t1_ref, xs_ref, conv_taps(pd, pw, 1))
        grad_ref[n] = tap_sum(t2t_ref, ogs_ref, spread_taps(pd, pw))


def first_kernel(
    xs_ref, pre_ref, ga_ref, og_ref, cross_ref, pair_ref, cls_ref, og_cols_ref, bias_ref, t1h_ref,
    t2th_ref,
    grads_ref, gp_ref, act_ref,
    rim_ref, ogs_ref, own_ref,
):
    j = lax.axis_index("sx")
    t = lax.axis_index("sy")
    low = t > 0
    high = t < NY - 1
    even = lax.rem(t, 2) == 0
    none = jnp.zeros((64, 128), BF16)
    ups = [jnp.where(even, cross_ref[s], pair_ref[s]) for s in range(NX)]
    downs = [jnp.where(even, pair_ref[s], cross_ref[s]) for s in range(NX)]
    ups = [jnp.where(low, x, none) for x in ups]
    downs = [jnp.where(high, x, none) for x in downs]
    rims = [jnp.concatenate([x, y], axis=0) for x, y in zip(ups, downs)]
    uses = [
        (n, tap, at) for n, (pd, pw) in enumerate(CLASSES) for tap, at in conv_taps(pd, pw, 1)
    ]
    for n, x in enumerate(by_class(rims, cls_ref[...])):
        forms = variants(x, CLASSES[n])
        for m, tap, at in uses:
            if at // 4 == n:
                rim_ref[m, tap * 128 : (tap + 1) * 128, :] = forms[at % 4]
    store_cotangents(ogs_ref, cotangents(rims, 2, og_cols_ref[...]))

    def with_rim(inner, outer):
        return jnp.concatenate(
            [inner[0:64] + outer[0:64], inner[64:256], inner[256:320] + outer[64:128]], axis=0
        )

    row = lax.broadcasted_iota(jnp.int32, (320, 256), 0)
    u = lax.rem(lax.broadcasted_iota(jnp.int32, (320, 256), 1), 32)
    row_ok = ((row >= 32) | low) & ((row < 288) | high)
    bias = bias_ref[...]
    for n, (pd, pw) in enumerate(CLASSES):
        pre = with_rim(pre_ref[n], dot(t1h_ref[...], rim_ref[n])) + bias
        local = 2 * u + pw
        wide = local + (32 * j - 2)
        ok = row_ok & (local >= 1) & (local <= 34) & (wide >= 0) & (wide < W)
        sigma = jax.nn.sigmoid(pre)
        act_ref[n] = jnp.where(ok, pre * sigma, 0.0).astype(BF16)
        grad = with_rim(ga_ref[n], tap_sum(t2th_ref, ogs_ref, spread_taps(pd, pw)))
        grad = jnp.where(ok, grad * sigma * (1.0 + pre * (1.0 - sigma)), 0.0)
        gp_ref[n] = grad.astype(BF16)
        mine = (u[32:288] >= 1) & (u[32:288] <= 16)
        own_ref[n] = jnp.where(mine, grad[32:288], 0.0).astype(BF16)

    lane = lax.rem(lax.broadcasted_iota(jnp.int32, (256, 256), 1), 32)
    og_own = jnp.where((lane >= 1) & (lane <= 16), og_ref[...].astype(F32), 0.0).astype(BF16)
    twos, ones = [], []
    for tap, (a, c) in enumerate(TAPS):
        twos.append(strip_sum(dot_nt(act_variant(act_ref, a, c), og_own), 4, 64))
        g = None
        for n, (pd, pw) in enumerate(CLASSES):
            at = variant(pd, pw, a - 1, c - 1)
            first = tap * 128 + 32
            x = jnp.concatenate(
                [
                    rim_ref[n, first : first + 32, :],
                    xs_ref[at],
                    rim_ref[n, first + 32 : first + 64, :],
                ],
                axis=0,
            )
            part = dot_nt(x, own_ref[n])
            g = part if g is None else g + part
        ones.append(strip_sum(g, 8, 32))
    twos.append(jnp.zeros((32, K), F32))
    ones.append(jnp.zeros((32, C), F32))
    twos = jnp.concatenate(twos, axis=0)
    ones = jnp.concatenate(ones, axis=0)
    twos = [twos[n * 128 : (n + 1) * 128].T for n in range(7)]
    ones = [ones[n * 128 : (n + 1) * 128].T for n in range(7)] + [jnp.zeros((C, 128), F32)] * 3
    for s in range(NX):
        for n in range(12):
            if n < 7:
                tile = twos[n][8 * s : 8 * s + 8]
            else:
                pair = ones[2 * n - 14], ones[2 * n - 13]
                tile = jnp.concatenate([x[4 * s : 4 * s + 4] for x in pair], axis=0)
            grads_ref[s * 2 + n // 6, n % 6 * 8 : n % 6 * 8 + 8, :] = tile


def act_variant(act_ref, a, c):
    pd, sd = step(0, a - 1)
    pw, sw = step(0, c - 1)
    x = act_ref[pd * 2 + pw]
    if sw:
        x = behind(x, 1)
    if sd:
        x = behind(x, 32)
    return x


def second_kernel(
    gp_ref, act_ref, k1_ref, k2_ref,
    out_ref, fcol_ref, rows_ref, og_rows_ref,
    gs_ref, t1t_ref, t2_ref,
):
    col = iota((1, 512), 1)
    half = (col >> 6) & 1
    gather_cols = from_row(
        1024, half * 512 + ((col >> 4) & 3) * 128 + (col >> 7) * 32 + 1 + (col & 15)
    )
    fcol_ref[...] = from_row(
        512,
        ((col >> 5) & 3) * 128
        + ((col >> 7) & 1) * 64
        + ((col >> 8) * 2 + (col & 1)) * 16
        + ((col & 31) >> 1),
    )
    col = col[:, 0:128]
    strided_cols = from_row(256, (col >> 4) * 32 + 1 + (col & 15))
    row = iota((256, 256), 0)
    col = iota((256, 256), 1)
    rows_ref[...] = pick(col == (row & 7) * 32 + (row >> 3))
    og_rows_ref[...] = pick(col == (row & ~31) + (row & 3) * 8 + ((row >> 2) & 7))
    build_back(k1_ref, k2_ref, t1t_ref, t2_ref)
    out = None
    for tap, (a, c) in enumerate(TAPS):
        part = dot(t2_ref[tap], act_variant(act_ref, a, c))
        out = part if out is None else out + part
    out = dot(out.astype(BF16), strided_cols)
    for s in range(NX):
        out_ref[s, 128:160, :] = jnp.concatenate(
            [out[g * 64 + 8 * s : g * 64 + 8 * s + 8] for g in range(4)], axis=0
        ).astype(BF16)
    for n, cls in enumerate(CLASSES):
        store_variants(gs_ref, gp_ref[n], cls)
    grads = [tap_sum(t1t_ref, gs_ref, conv_taps(pd, pw, -1)).astype(BF16) for pd, pw in CLASSES]
    for q in range(2):
        at = slice(q * 128, (q + 1) * 128)
        cat = jnp.concatenate(
            [grads[n][half * 128 : (half + 1) * 128, at] for half in range(2) for n in range(4)], axis=1
        )
        got = move(cat, gather_cols)
        for e in range(4):
            out_ref[4 * q + e, 0:128, :] = got[:, e * 128 : (e + 1) * 128]


def sum_kernel(r_ref, after_ref, out_ref):
    total = r_ref[0]
    for s in range(1, r_ref.shape[0]):
        total = total + r_ref[s]
    out_ref[...] = total


def pair_kernel(a_ref, b_ref, out_ref):
    total = a_ref[...] + b_ref[...]
    for n in range(out_ref.shape[0]):
        out_ref[n] = total


def append_kernel(mine_ref, other_ref, buf_ref, out_ref, two_ref):
    first = lax.rem(lax.axis_index("sy"), 2) == 0
    mine, other = mine_ref[...], other_ref[...]
    even = jnp.where(first, mine, other)
    odd = jnp.where(first, other, mine)
    total = jnp.concatenate([even, odd], axis=0)
    two_ref[...] = total[0:56]
    one = total[56:96]
    hi = one.astype(BF16).astype(F32)
    both = jnp.concatenate([hi, one - hi], axis=0).astype(BF16)
    for s in range(NX):
        out_ref[s] = both


def last_kernel(
    r_ref, g_ref, fcol_ref, rows_ref, og_rows_ref,
    strided_ref, two_ref, one_ref, vol_ref, *, out_scale, in_scale,
):
    halves = []
    for q in range(2):
        cat = jnp.concatenate([r_ref[4 * q + s, 0:128, :] for s in range(4)], axis=1)
        halves.append(move(cat, fcol_ref[...]))
    for pd in range(2):
        blocks = []
        for half in range(2):
            at = slice((pd * 2 + half) * 128, (pd * 2 + half + 1) * 128)
            blocks.append(jnp.concatenate([halves[0][:, at], halves[1][:, at]], axis=1))
        vol_ref[pd * 256 : (pd + 1) * 256, :] = move(rows_ref[...], jnp.concatenate(blocks, axis=0))
    parts = [r_ref[s, 128:160, :].astype(F32) for s in range(NX)]
    group = iota((32, 128), 1) >> 4
    blocks = []
    for e in range(8):
        block = None
        for j in range(NX):
            turned = pltpu.roll(parts[j], (j - e) * 16 % 128, 1) if j != e else parts[j]
            block = turned if block is None else jnp.where(group == j, turned, block)
        blocks.append(block)
    strided_ref[...] = move(og_rows_ref[...], jnp.concatenate(blocks, axis=0).astype(BF16))
    sums = [r_ref[s, 160:200, :].astype(F32) + r_ref[s, 200:240, :].astype(F32) for s in range(NX)]
    two = g_ref[...] * out_scale
    for n in range(7):
        one = jnp.concatenate([x[4 * n : 4 * n + 4] for x in sums], axis=0) * in_scale
        for m in range(4 * n, min(4 * n + 4, 27)):
            a, c = TAPS[m // 3]
            tap = a * 9 + m % 3 * 3 + c
            at = slice((m - 4 * n) * 32, (m - 4 * n + 1) * 32)
            one_ref[tap] = one[:, at]
            two_ref[tap] = two[n * 8 : (n + 1) * 8, at]


def call(body, outs, args, scratch=(), specs=None, out_specs=None, aliases=None, grid=(), us=1, vmem=16):
    return pl.pallas_call(
        body,
        out_shape=outs,
        grid=grid,
        in_specs=specs or [pl.BlockSpec(memory_space=pltpu.VMEM)] * len(args),
        out_specs=out_specs or jax.tree.map(lambda _: pl.BlockSpec(memory_space=pltpu.VMEM), outs),
        scratch_shapes=list(scratch),
        input_output_aliases=aliases or {},
        compiler_params=pltpu.CompilerParams(vmem_limit_bytes=vmem * 1024 * 1024),
        cost_estimate=pl.CostEstimate(flops=us * 10**9, bytes_accessed=0, transcendentals=0),
    )(*args)


def whole(*dims):
    return pl.BlockSpec(dims, lambda n: (0,) * len(dims))


def shape(*dims, dtype=BF16):
    return jax.ShapeDtypeStruct(dims, dtype)


def per_device(volume, kernel_one, bias_one, kernel_two, out_grad):
    out_scale = (8 * 128 * 128) ** (-0.5)
    in_scale = (16 * 256 * 256) ** (-0.5)
    chunks = call(
        pack_kernel,
        shape(NX, 256, 128),
        (volume.reshape(512, 256), out_grad.reshape(256, 128)),
        specs=[pl.BlockSpec(memory_space=pl.ANY)] * 2,
        out_specs=pl.BlockSpec(memory_space=pl.ANY),
        scratch=(
            pltpu.VMEM((512, 256), BF16),
            pltpu.VMEM((256, 128), BF16),
            pltpu.VMEM((NX, 256, 128), BF16),
            pltpu.SemaphoreType.DMA((2 + NX,)),
        ),
        vmem=60,
    )
    got = lax.all_to_all(chunks, "sx", 0, 0)
    k1 = kernel_one.transpose(2, 3, 4, 0, 1).reshape(27, C, C)
    k2 = kernel_two.transpose(2, 3, 4, 1, 0).reshape(27, C, K)
    strips, even, odd, class_cols, og_cols = call(
        weights_kernel,
        (
            shape(9, 4, 32, 256), shape(9, 2, 32, 256), shape(9, 2, 32, 128),
            shape(512, 512), shape(1024, 256),
        ),
        (k1, k2),
        us=3,
    )
    bias = jnp.tile(bias_one.astype(F32), 10)[:, None]
    cross, pair = call(split_kernel, (shape(NX, 64, 128), shape(NX, 64, 128)), (got,))
    k1, k2, cross = lax.optimization_barrier((k1, k2, cross))
    t1h, t2th = call(rim_kernel, (shape(128, 9 * 128), shape(9, 128, 128)), (k1, k2))
    ends = (0, NY - 1)
    cross = lax.ppermute(
        cross, "sy", [(i, i if i in ends else ((i - 1) ^ 1) + 1) for i in range(NY)]
    )
    pair = lax.ppermute(pair, "sy", [(i, i ^ 1) for i in range(NY)])
    og, xs, pre, grad_act = call(
        inner_kernel,
        (shape(256, 256), shape(16, 256, 256), shape(4, 320, 256, dtype=F32), shape(4, 320, 256, dtype=F32)),
        (got, class_cols, og_cols, strips, even, odd),
        scratch=(
            pltpu.VMEM((4, 256, 256), BF16),
            pltpu.VMEM((9, 320, 256), BF16),
            pltpu.VMEM((9, 320, 256), BF16),
        ),
        us=5,
    )
    grads, gp, act = call(
        first_kernel,
        (shape(2 * NX, 48, 128, dtype=F32), shape(4, 320, 256), shape(4, 320, 256)),
        (xs, pre, grad_act, og, cross, pair, class_cols, og_cols, bias, t1h, t2th),
        scratch=(
            pltpu.VMEM((4, 9 * 128, 256), BF16),
            pltpu.VMEM((4, 128, 256), BF16),
            pltpu.VMEM((4, 256, 256), BF16),
        ),
        us=5,
    )
    grads = lax.all_to_all(
        grads,
        ("sx", "sy"),
        0,
        0,
        axis_index_groups=[
            [s * NY + 2 * q + r for s in range(NX) for r in range(2)] for q in range(NY // 2)
        ],
    )
    buffer, plane_cols, rows_back, og_rows_back = call(
        second_kernel,
        (shape(NX, 240, 128), shape(512, 512), shape(256, 256), shape(256, 256)),
        (gp, act, k1, k2),
        scratch=(
            pltpu.VMEM((16, 320, 256), BF16),
            pltpu.VMEM((9, 256, 320), BF16),
            pltpu.VMEM((9, 256, 320), BF16),
        ),
        us=6,
        vmem=20,
    )
    both = [pl.BlockSpec(memory_space=pltpu.VMEM), pl.BlockSpec(memory_space=pl.ANY)]
    keep = call(sum_kernel, shape(48, 128, dtype=F32), (grads, buffer), specs=both)
    keep = call(
        pair_kernel,
        shape(8, 48, 128, dtype=F32),
        (keep, lax.ppermute(keep, "sy", [(i, i ^ 2) for i in range(NY)])),
    )
    keep = lax.all_to_all(
        keep, "sy", 0, 0, axis_index_groups=[[4 * z + r for z in (0, 4, 2, 6, 1, 5, 3, 7)] for r in range(4)]
    )
    keep = call(sum_kernel, shape(48, 128, dtype=F32), (keep, buffer), specs=both)
    other = lax.ppermute(keep, "sy", [(i, i ^ 1) for i in range(NY)])
    buffer, two = call(
        append_kernel,
        (shape(NX, 240, 128), shape(56, 128, dtype=F32)),
        (keep, other, buffer),
        specs=[whole(48, 128), whole(48, 128), pl.BlockSpec(memory_space=pl.ANY)],
        out_specs=(pl.BlockSpec((NX, 80, 128), lambda n: (0, 2, 0)), whole(56, 128)),
        grid=(1,),
        aliases={2: 0},
    )
    got = lax.all_to_all(buffer, "sx", 0, 0)
    strided, two, one, vol = call(
        functools.partial(last_kernel, out_scale=out_scale, in_scale=in_scale),
        (shape(256, 128), shape(27, 8, C, dtype=F32), shape(27, C, C, dtype=F32), shape(512, 256)),
        (got, two, plane_cols, rows_back, og_rows_back),
    )
    return (
        strided.reshape(8, 8, 4, 128),
        two.reshape(3, 3, 3, 8, C).transpose(3, 4, 0, 1, 2),
        one.reshape(3, 3, 3, C, C).transpose(3, 4, 0, 1, 2),
        vol.reshape(2, C, 8, W),
    )


def solution(mesh):
    return jax.shard_map(
        per_device,
        mesh=mesh,
        in_specs=(P("sx", None, "sy", None), P(), P(), P(), P(None, "sx", "sy", None)),
        out_specs=(
            P(None, "sx", "sy", None),
            P("sx", None, None, None, None),
            P(),
            P("sx", None, "sy", None),
        ),
        check_vma=False,
    )
```

```python
import functools

import jax
import jax.numpy as jnp
from jax import lax
from jax.experimental import pallas as pl
from jax.experimental.pallas import tpu as pltpu
from jax.sharding import PartitionSpec as P

F32 = jnp.float32
BF16 = jnp.bfloat16
NX = 8
NY = 32
C = 32
K = 64
W = 256
CLASSES = ((0, 0), (0, 1), (1, 0), (1, 1))
TAPS = tuple((a, c) for a in range(3) for c in range(3))


def iota(dims, axis):
    return lax.broadcasted_iota(jnp.int32, dims, axis)


def pick(mask):
    return jnp.where(mask, 1.0, 0.0).astype(BF16)


def dot(a, b):
    return jnp.dot(a, b, preferred_element_type=F32)


def move(a, b):
    return dot(a, b).astype(BF16)


def dot_nt(a, b):
    return lax.dot_general(a, b, (((1,), (1,)), ((), ())), preferred_element_type=F32)


def ahead(x, n):
    return jnp.concatenate([x[:, n:], jnp.zeros((x.shape[0], n), x.dtype)], axis=1)


def behind(x, n):
    return jnp.concatenate([jnp.zeros((x.shape[0], n), x.dtype), x[:, :-n]], axis=1)


def step(parity, offset):
    at = parity + offset
    return (1, 1) if at == -1 else (0, 1) if at == 2 else (at, 0)


def variant(pd, pw, da, dc):
    qd, sd = step(pd, da)
    qw, sw = step(pw, dc)
    return ((qd * 2 + qw) * 2 + sd) * 2 + sw


def variants(x, cls):
    move_d = behind if cls[0] else ahead
    move_w = behind if cls[1] else ahead
    along = move_w(x, 1)
    return x, along, move_d(x, 32), move_d(along, 32)


def store_variants(ref, x, cls):
    base = (cls[0] * 2 + cls[1]) * 4
    for n, form in enumerate(variants(x, cls)):
        ref[base + n] = form


def width_block(n):
    flip = lax.rem(lax.axis_index("sy") // 2, 2)
    return n + (1 - 2 * (n % 2)) * flip


def pack_kernel(vol_hbm, og_hbm, out_hbm, vol_ref, og_ref, out_ref, sems):
    copies = (
        pltpu.make_async_copy(vol_hbm, vol_ref, sems.at[0]),
        pltpu.make_async_copy(og_hbm, og_ref, sems.at[1]),
    )
    for copy in copies:
        copy.start()
    row = iota((256, 256), 0)
    col = iota((256, 256), 1)
    by_row = pick(col == (row & 31) * 8 + (row >> 5))
    by_kind = pick(col == ((row >> 3) & 7) * 32 + (row & 7) * 4 + (row >> 6))
    lane = iota((1, 128), 1)
    cls = jnp.where(lane >= 20, 1, 0) + jnp.where(lane >= 40, 1, 0) + jnp.where(lane >= 60, 1, 0)
    u = lane - 20 * cls
    at = iota((128, 128), 0)
    chosen = []
    for j in range(NX):
        w = jnp.where((lane < 80) & (u < 18), 32 * j - 2 + 2 * u + (cls & 1), -1)
        pieces = []
        for pd in range(2):
            from_plane = jnp.where(cls >> 1 == pd, w, -1)
            for block in range(max(0, 32 * j - 2) // 128, min(W - 1, 32 * j + 33) // 128 + 1):
                pieces.append((pd, block, pick(at + 128 * block == from_plane)))
        g = jnp.where((lane >= 80) & (lane < 98), 16 * j - 1 + lane - 80, -1)
        pieces.append((2, 0, pick(at == g)))
        chosen.append(pieces)
    for copy in copies:
        copy.wait()
    planes = (
        move(by_row, vol_ref[0:256]),
        move(by_row, vol_ref[256:512]),
        move(by_kind, og_ref[...]),
    )
    for j in range(NX):
        cat = jnp.concatenate(
            [planes[n][:, block * 128 : (block + 1) * 128] for n, block, _ in chosen[j]], axis=1
        )
        out_ref[j] = move(cat, jnp.concatenate([m for _, _, m in chosen[j]], axis=0))
        copies += (pltpu.make_async_copy(out_ref.at[j], out_hbm.at[width_block(j)], sems.at[2 + j]),)
        copies[-1].start()
    for copy in copies[2:]:
        copy.wait()


def split_kernel(r_ref, cross_ref, pair_ref):
    for s in range(NX):
        cross_ref[s] = r_ref[s, 192:256, :]
        pair_ref[s] = r_ref[s, 0:64, :]


def by_class(parts, cls_cols):
    got = [move(jnp.concatenate(parts[4 * q : 4 * q + 4], axis=1), cls_cols) for q in range(2)]
    return [
        jnp.concatenate([x[:, n * 128 : (n + 1) * 128] for x in got], axis=1) for n in range(4)
    ]


def cotangents(parts, groups, og_cols):
    parts = [x.astype(F32) for x in parts]
    cat = [
        jnp.concatenate(
            [x[g * 64 + e * 8 : g * 64 + e * 8 + 8] for g in range(groups) for x in parts], axis=0
        )
        for e in range(8)
    ]
    return move(jnp.concatenate(cat, axis=1).astype(BF16), og_cols)


def place(strip, offset, width):
    if offset >= width:
        return jnp.zeros((strip.shape[0], width), strip.dtype)
    first = max(0, -offset)
    strip = strip[:, first : min(strip.shape[1], width - offset)]
    offset += first
    parts = [strip]
    if offset:
        parts.insert(0, jnp.zeros((strip.shape[0], offset), strip.dtype))
    rest = width - offset - strip.shape[1]
    if rest:
        parts.append(jnp.zeros((strip.shape[0], rest), strip.dtype))
    return jnp.concatenate(parts, axis=1)


def from_row(rows, target):
    return pick(iota((rows, target.shape[1]), 0) == target)


def kernel_blocks(ref, a, c):
    return [ref[a * 9 + b * 3 + c].astype(F32) for b in range(3)]


def weights_kernel(
    k1_ref, k2_ref, strips_ref, even_ref, odd_ref, cls_ref, og_cols_ref
):
    col = iota((1, 512), 1)
    u = col & 31
    cls_ref[...] = from_row(512, jnp.where(u < 18, ((col >> 5) & 3) * 128 + (col >> 7) * 20 + u, -1))
    col, u = col[:, 0:256], u[:, 0:256]
    og_cols_ref[...] = from_row(1024, jnp.where(u < 18, (col >> 5) * 128 + 80 + u, -1))
    for t, (a, c) in enumerate(TAPS):
        k1 = kernel_blocks(k1_ref, a, c)
        k2 = kernel_blocks(k2_ref, a, c)
        forward = jnp.concatenate(k1, axis=1)
        even = jnp.concatenate([k2[2], k2[0]], axis=1)
        for r in range(4):
            strips_ref[t, r] = place(forward, 32 * r, 256).astype(BF16)
        for r in range(2):
            even_ref[t, r] = place(even, 64 * r, 256).astype(BF16)
            odd_ref[t, r] = place(k2[1], 64 * r, 128).astype(BF16)


def rim_kernel(k1_ref, k2_ref, t1h_ref, t2th_ref):
    gap = jnp.zeros((C, C), F32)
    wide = jnp.zeros((C, K), F32)
    for t, (a, c) in enumerate(TAPS):
        k1 = kernel_blocks(k1_ref, a, c)
        k2 = kernel_blocks(k2_ref, a, c)
        rim = (
            (k1[0], k1[1], gap, gap),
            (gap, k1[0], gap, gap),
            (gap, gap, k1[2], gap),
            (gap, gap, k1[1], k1[2]),
        )
        t1h_ref[:, t * 128 : (t + 1) * 128] = jnp.concatenate(
            [jnp.concatenate(r, axis=1) for r in rim], axis=0
        ).astype(BF16)
        rim = ((k2[2], wide), (wide, wide), (wide, k2[0]), (wide, k2[1]))
        t2th_ref[t] = jnp.concatenate([jnp.concatenate(r, axis=1) for r in rim], axis=0).astype(BF16)


def window(strip, at):
    if at == 0:
        return strip
    none = jnp.zeros((strip.shape[0], 128), strip.dtype)
    return jnp.concatenate([strip[:, 128:], none] if at < 0 else [none, strip[:, :128]], axis=1)


def build_forward(strips_ref, even_ref, odd_ref, t1_ref, t2t_ref):
    none = jnp.zeros((C, 128), BF16)
    for t in range(9):
        for h in range(10):
            at = slice(h * 32, (h + 1) * 32)
            r = (h + 2) % 4
            t1_ref[t, at, :] = window(strips_ref[t, r], (h - 2 - r) // 4)
            if h % 2 == 0:
                r = (h // 2 + 1) % 2
                t2t_ref[t, at, :] = window(even_ref[t, r], (h // 2 - 1 - r) // 2)
            else:
                n = h // 2
                strip = odd_ref[t, n % 2] if n < 4 else none
                t2t_ref[t, at, :] = jnp.concatenate([none, strip] if n > 1 else [strip, none], axis=1)


def build_back(k1_ref, t1t_ref):
    for t, (a, c) in enumerate(TAPS):
        back = jnp.concatenate([x.T for x in reversed(kernel_blocks(k1_ref, a, c))], axis=1)
        for h in range(8):
            t1t_ref[t, h * 32 : (h + 1) * 32, :] = place(back, 32 * h, 320).astype(BF16)


def build_strided(k2_ref, t2_ref):
    for t, (a, c) in enumerate(TAPS):
        strided = jnp.concatenate([x.T for x in kernel_blocks(k2_ref, a, c)], axis=1)
        for g in range(4):
            t2_ref[t, g * 64 : (g + 1) * 64, :] = place(strided, 64 * g, 320).astype(BF16)


def strip_sum(g, blocks, jump):
    width = g.shape[1] // blocks
    total = None
    for n in range(blocks):
        part = g[n * jump : n * jump + 96, n * width : (n + 1) * width]
        total = part if total is None else total + part
    return total


def conv_taps(pd, pw, sign):
    return [(tap, variant(pd, pw, sign * (a - 1), sign * (c - 1))) for tap, (a, c) in enumerate(TAPS)]


def spread_taps(pd, pw):
    depth = ((1, 0),) if pd == 0 else ((2, 0), (0, 1))
    width = ((1, 0),) if pw == 0 else ((2, 0), (0, 1))
    return [(a * 3 + c, sd * 2 + sw) for a, sd in depth for c, sw in width]


def tap_sum(weights_ref, inputs_ref, pairs):
    total = None
    for tap, at in pairs:
        part = dot(weights_ref[tap], inputs_ref[at])
        total = part if total is None else total + part
    return total


def store_cotangents(ref, og):
    along = ahead(og, 1)
    ref[0] = og
    ref[1] = along
    ref[2] = ahead(og, 32)
    ref[3] = ahead(along, 32)


def inner_kernel(
    r_ref, cls_ref, og_cols_ref, strips_ref, even_ref, odd_ref,
    og_ref, xs_ref, pre_ref, grad_ref,
    ogs_ref, t1_ref, t2t_ref,
):
    build_forward(strips_ref, even_ref, odd_ref, t1_ref, t2t_ref)
    parts = [r_ref[s] for s in range(NX)]
    for x, cls in zip(by_class(parts, cls_ref[...]), CLASSES):
        store_variants(xs_ref, x, cls)
    og_ref[...] = cotangents(parts, 4, og_cols_ref[...])
    store_cotangents(ogs_ref, og_ref[...])
    for n, (pd, pw) in enumerate(CLASSES):
        pre_ref[n] = tap_sum(t1_ref, xs_ref, conv_taps(pd, pw, 1))
        grad_ref[n] = tap_sum(t2t_ref, ogs_ref, spread_taps(pd, pw))


def first_kernel(
    xs_ref, pre_ref, ga_ref, og_ref, cross_ref, pair_ref, cls_ref, og_cols_ref, bias_ref, t1h_ref,
    t2th_ref,
    grads_ref, gp_ref, act_ref,
    rim_ref, ogs_ref, own_ref,
):
    j = width_block(lax.axis_index("sx"))
    t = lax.axis_index("sy")
    low = t > 0
    high = t < NY - 1
    none = jnp.zeros((64, 128), BF16)
    ups = [cross_ref[s] for s in range(NX)]
    downs = [pair_ref[s] for s in range(NX)]
    ups = [jnp.where(low, x, none) for x in ups]
    downs = [jnp.where(high, x, none) for x in downs]
    rims = [jnp.concatenate([x, y], axis=0) for x, y in zip(ups, downs)]
    uses = [
        (n, tap, at) for n, (pd, pw) in enumerate(CLASSES) for tap, at in conv_taps(pd, pw, 1)
    ]
    for n, x in enumerate(by_class(rims, cls_ref[...])):
        forms = variants(x, CLASSES[n])
        for m, tap, at in uses:
            if at // 4 == n:
                rim_ref[m, tap * 128 : (tap + 1) * 128, :] = forms[at % 4]
    store_cotangents(ogs_ref, cotangents(rims, 2, og_cols_ref[...]))

    def with_rim(inner, outer):
        return jnp.concatenate(
            [inner[0:64] + outer[0:64], inner[64:256], inner[256:320] + outer[64:128]], axis=0
        )

    row = lax.broadcasted_iota(jnp.int32, (320, 256), 0)
    u = lax.rem(lax.broadcasted_iota(jnp.int32, (320, 256), 1), 32)
    row_ok = ((row >= 32) | low) & ((row < 288) | high)
    bias = bias_ref[...]
    for n, (pd, pw) in enumerate(CLASSES):
        pre = with_rim(pre_ref[n], dot(t1h_ref[...], rim_ref[n])) + bias
        local = 2 * u + pw
        wide = local + (32 * j - 2)
        ok = row_ok & (local >= 1) & (local <= 34) & (wide >= 0) & (wide < W)
        sigma = jax.nn.sigmoid(pre)
        act_ref[n] = jnp.where(ok, pre * sigma, 0.0).astype(BF16)
        grad = with_rim(ga_ref[n], tap_sum(t2th_ref, ogs_ref, spread_taps(pd, pw)))
        grad = jnp.where(ok, grad * sigma * (1.0 + pre * (1.0 - sigma)), 0.0)
        gp_ref[n] = grad.astype(BF16)
        mine = (u[32:288] >= 1) & (u[32:288] <= 16)
        own_ref[n] = jnp.where(mine, grad[32:288], 0.0).astype(BF16)

    lane = lax.rem(lax.broadcasted_iota(jnp.int32, (256, 256), 1), 32)
    og_own = jnp.where((lane >= 1) & (lane <= 16), og_ref[...].astype(F32), 0.0).astype(BF16)
    twos, ones = [], []
    for tap, (a, c) in enumerate(TAPS):
        twos.append(strip_sum(dot_nt(act_variant(act_ref, a, c), og_own), 4, 64))
        g = None
        for n, (pd, pw) in enumerate(CLASSES):
            at = variant(pd, pw, a - 1, c - 1)
            first = tap * 128 + 32
            x = jnp.concatenate(
                [
                    rim_ref[n, first : first + 32, :],
                    xs_ref[at],
                    rim_ref[n, first + 32 : first + 64, :],
                ],
                axis=0,
            )
            part = dot_nt(x, own_ref[n])
            g = part if g is None else g + part
        ones.append(strip_sum(g, 8, 32))
    twos.append(jnp.zeros((32, K), F32))
    ones.append(jnp.zeros((32, C), F32))
    twos = jnp.concatenate(twos, axis=0)
    ones = jnp.concatenate(ones, axis=0)
    twos = [twos[n * 128 : (n + 1) * 128].T for n in range(7)]
    ones = [ones[n * 128 : (n + 1) * 128].T for n in range(7)] + [jnp.zeros((C, 128), F32)] * 3
    for s in range(NX):
        for n in range(12):
            if n < 7:
                tile = twos[n][8 * s : 8 * s + 8]
            else:
                pair = ones[2 * n - 14], ones[2 * n - 13]
                tile = jnp.concatenate([x[4 * s : 4 * s + 4] for x in pair], axis=0)
            grads_ref[s * 2 + n // 6, n % 6 * 8 : n % 6 * 8 + 8, :] = tile


def act_variant(act_ref, a, c):
    pd, sd = step(0, a - 1)
    pw, sw = step(0, c - 1)
    x = act_ref[pd * 2 + pw]
    if sw:
        x = behind(x, 1)
    if sd:
        x = behind(x, 32)
    return x


def strided_kernel(act_ref, k2_ref, out_ref, t2_ref):
    build_strided(k2_ref, t2_ref)
    col = iota((1, 128), 1)
    strided_cols = from_row(256, (col >> 4) * 32 + 1 + (col & 15))
    out = None
    for tap, (a, c) in enumerate(TAPS):
        part = dot(t2_ref[tap], act_variant(act_ref, a, c))
        out = part if out is None else out + part
    out = dot(out.astype(BF16), strided_cols)
    for s in range(NX):
        out_ref[s] = jnp.concatenate(
            [out[g * 64 + 8 * s : g * 64 + 8 * s + 8] for g in range(4)], axis=0
        ).astype(BF16)


def second_kernel(
    gp_ref, k1_ref, strided_ref,
    out_ref, fcol_ref, rows_ref, og_rows_ref,
    gs_ref, t1t_ref,
):
    col = iota((1, 512), 1)
    half = (col >> 6) & 1
    gather_cols = from_row(
        1024, half * 512 + ((col >> 4) & 3) * 128 + (col >> 7) * 32 + 1 + (col & 15)
    )
    fcol_ref[...] = from_row(
        512,
        ((col >> 5) & 3) * 128
        + ((col >> 7) & 1) * 64
        + ((col >> 8) * 2 + (col & 1)) * 16
        + ((col & 31) >> 1),
    )
    row = iota((256, 256), 0)
    col = iota((256, 256), 1)
    rows_ref[...] = pick(col == (row & 7) * 32 + (row >> 3))
    og_rows_ref[...] = pick(col == (row & ~31) + (row & 3) * 8 + ((row >> 2) & 7))
    build_back(k1_ref, t1t_ref)
    for n, cls in enumerate(CLASSES):
        store_variants(gs_ref, gp_ref[n], cls)
    grads = [tap_sum(t1t_ref, gs_ref, conv_taps(pd, pw, -1)).astype(BF16) for pd, pw in CLASSES]
    for q in range(2):
        at = slice(q * 128, (q + 1) * 128)
        cat = jnp.concatenate(
            [grads[n][half * 128 : (half + 1) * 128, at] for half in range(2) for n in range(4)], axis=1
        )
        got = move(cat, gather_cols)
        for e in range(4):
            out_ref[4 * q + e, 0:128, :] = got[:, e * 128 : (e + 1) * 128]
    for s in range(NX):
        out_ref[s, 128:160, :] = strided_ref[s]


def first_sum_kernel(r_ref, out_ref):
    total = r_ref[0]
    for s in range(1, r_ref.shape[0]):
        total = total + r_ref[s]
    out_ref[...] = total


def sum_kernel(r_ref, after_ref, out_ref):
    total = r_ref[0]
    for s in range(1, r_ref.shape[0]):
        total = total + r_ref[s]
    out_ref[...] = total


def pair_kernel(a_ref, b_ref, after_ref, out_ref):
    total = a_ref[...] + b_ref[...]
    for n in range(out_ref.shape[0]):
        out_ref[n] = total


def append_kernel(mine_ref, other_ref, buf_ref, out_ref, two_ref):
    first = lax.rem(lax.axis_index("sy"), 2) == 0
    mine, other = mine_ref[...], other_ref[...]
    even = jnp.where(first, mine, other)
    odd = jnp.where(first, other, mine)
    total = jnp.concatenate([even, odd], axis=0)
    two_ref[...] = total[0:56]
    one = total[56:96]
    hi = one.astype(BF16).astype(F32)
    both = jnp.concatenate([hi, one - hi], axis=0).astype(BF16)
    for s in range(NX):
        out_ref[s] = both


def last_kernel(
    r_ref, g_ref, fcol_ref, rows_ref, og_rows_ref,
    strided_ref, two_ref, one_ref, vol_ref, *, out_scale, in_scale,
):
    halves = []
    for q in range(2):
        cat = jnp.concatenate([r_ref[width_block(4 * q + s), 0:128, :] for s in range(4)], axis=1)
        halves.append(move(cat, fcol_ref[...]))
    for pd in range(2):
        blocks = []
        for half in range(2):
            at = slice((pd * 2 + half) * 128, (pd * 2 + half + 1) * 128)
            blocks.append(jnp.concatenate([halves[0][:, at], halves[1][:, at]], axis=1))
        vol_ref[pd * 256 : (pd + 1) * 256, :] = move(rows_ref[...], jnp.concatenate(blocks, axis=0))
    parts = [r_ref[width_block(s), 128:160, :].astype(F32) for s in range(NX)]
    group = iota((32, 128), 1) >> 4
    blocks = []
    for e in range(8):
        block = None
        for j in range(NX):
            turned = pltpu.roll(parts[j], (j - e) * 16 % 128, 1) if j != e else parts[j]
            block = turned if block is None else jnp.where(group == j, turned, block)
        blocks.append(block)
    strided_ref[...] = move(og_rows_ref[...], jnp.concatenate(blocks, axis=0).astype(BF16))
    sums = [r_ref[s, 160:200, :].astype(F32) + r_ref[s, 200:240, :].astype(F32) for s in range(NX)]
    two = g_ref[...] * out_scale
    for n in range(7):
        one = jnp.concatenate([x[4 * n : 4 * n + 4] for x in sums], axis=0) * in_scale
        for m in range(4 * n, min(4 * n + 4, 27)):
            a, c = TAPS[m // 3]
            tap = a * 9 + m % 3 * 3 + c
            at = slice((m - 4 * n) * 32, (m - 4 * n + 1) * 32)
            one_ref[tap] = one[:, at]
            two_ref[tap] = two[n * 8 : (n + 1) * 8, at]


def call(body, outs, args, scratch=(), specs=None, out_specs=None, aliases=None, grid=(), us=1, vmem=16):
    return pl.pallas_call(
        body,
        out_shape=outs,
        grid=grid,
        in_specs=specs or [pl.BlockSpec(memory_space=pltpu.VMEM)] * len(args),
        out_specs=out_specs or jax.tree.map(lambda _: pl.BlockSpec(memory_space=pltpu.VMEM), outs),
        scratch_shapes=list(scratch),
        input_output_aliases=aliases or {},
        compiler_params=pltpu.CompilerParams(vmem_limit_bytes=vmem * 1024 * 1024),
        cost_estimate=pl.CostEstimate(flops=us * 10**9, bytes_accessed=0, transcendentals=0),
    )(*args)


def whole(*dims):
    return pl.BlockSpec(dims, lambda n: (0,) * len(dims))


def shape(*dims, dtype=BF16):
    return jax.ShapeDtypeStruct(dims, dtype)


def per_device(volume, kernel_one, bias_one, kernel_two, out_grad):
    out_scale = (8 * 128 * 128) ** (-0.5)
    in_scale = (16 * 256 * 256) ** (-0.5)
    chunks = call(
        pack_kernel,
        shape(NX, 256, 128),
        (volume.reshape(512, 256), out_grad.reshape(256, 128)),
        specs=[pl.BlockSpec(memory_space=pl.ANY)] * 2,
        out_specs=pl.BlockSpec(memory_space=pl.ANY),
        scratch=(
            pltpu.VMEM((512, 256), BF16),
            pltpu.VMEM((256, 128), BF16),
            pltpu.VMEM((NX, 256, 128), BF16),
            pltpu.SemaphoreType.DMA((2 + NX,)),
        ),
        vmem=60,
    )
    got = lax.all_to_all(chunks, "sx", 0, 0)
    k1 = kernel_one.transpose(2, 3, 4, 0, 1).reshape(27, C, C)
    k2 = kernel_two.transpose(2, 3, 4, 1, 0).reshape(27, C, K)
    strips, even, odd, class_cols, og_cols = call(
        weights_kernel,
        (
            shape(9, 4, 32, 256), shape(9, 2, 32, 256), shape(9, 2, 32, 128),
            shape(512, 512), shape(1024, 256),
        ),
        (k1, k2),
        us=3,
    )
    bias = jnp.tile(bias_one.astype(F32), 10)[:, None]
    cross, pair = call(split_kernel, (shape(NX, 64, 128), shape(NX, 64, 128)), (got,))
    k1, k2, cross = lax.optimization_barrier((k1, k2, cross))
    t1h, t2th = call(rim_kernel, (shape(128, 9 * 128), shape(9, 128, 128)), (k1, k2))
    up = [
        (s * NY + t, (s ^ (t % 2)) * NY + (t + 1) % NY) for s in range(NX) for t in range(NY)
    ]
    cross = lax.ppermute(cross, ("sx", "sy"), up)
    pair = lax.ppermute(pair, ("sx", "sy"), [(b, a) for a, b in up])
    og, xs, pre, grad_act = call(
        inner_kernel,
        (shape(256, 256), shape(16, 256, 256), shape(4, 320, 256, dtype=F32), shape(4, 320, 256, dtype=F32)),
        (got, class_cols, og_cols, strips, even, odd),
        scratch=(
            pltpu.VMEM((4, 256, 256), BF16),
            pltpu.VMEM((9, 320, 256), BF16),
            pltpu.VMEM((9, 320, 256), BF16),
        ),
        us=5,
    )
    grads, gp, act = call(
        first_kernel,
        (shape(2 * NX, 48, 128, dtype=F32), shape(4, 320, 256), shape(4, 320, 256)),
        (xs, pre, grad_act, og, cross, pair, class_cols, og_cols, bias, t1h, t2th),
        scratch=(
            pltpu.VMEM((4, 9 * 128, 256), BF16),
            pltpu.VMEM((4, 128, 256), BF16),
            pltpu.VMEM((4, 256, 256), BF16),
        ),
        us=5,
    )
    grads = lax.all_to_all(
        grads,
        ("sx", "sy"),
        0,
        0,
        axis_index_groups=[
            [s * NY + 2 * q + r for s in range(NX) for r in range(2)] for q in range(NY // 2)
        ],
    )
    both = [pl.BlockSpec(memory_space=pltpu.VMEM), pl.BlockSpec(memory_space=pl.ANY)]
    keep = call(first_sum_kernel, shape(48, 128, dtype=F32), (grads,))
    keep, act = lax.optimization_barrier((keep, act))
    other = lax.ppermute(keep, "sy", [(i, i ^ 2) for i in range(NY)])
    strided = call(
        strided_kernel,
        shape(NX, 32, 128),
        (act, k2),
        scratch=(pltpu.VMEM((9, 256, 320), BF16),),
        us=2,
    )
    keep = call(
        pair_kernel,
        shape(8, 48, 128, dtype=F32),
        (keep, other, strided),
        specs=[pl.BlockSpec(memory_space=pltpu.VMEM)] + both,
    )
    keep, gp = lax.optimization_barrier((keep, gp))
    buffer, plane_cols, rows_back, og_rows_back = call(
        second_kernel,
        (shape(NX, 240, 128), shape(512, 512), shape(256, 256), shape(256, 256)),
        (gp, k1, strided),
        scratch=(pltpu.VMEM((16, 320, 256), BF16), pltpu.VMEM((9, 256, 320), BF16)),
        us=5,
        vmem=20,
    )
    keep = lax.all_to_all(
        keep,
        "sy",
        0,
        0,
        axis_index_groups=[[4 * z + r for z in (0, 4, 2, 6, 1, 5, 3, 7)] for r in range(4)],
    )
    keep = call(sum_kernel, shape(48, 128, dtype=F32), (keep, buffer), specs=both)
    other = lax.ppermute(keep, "sy", [(i, i ^ 1) for i in range(NY)])
    buffer, two = call(
        append_kernel,
        (shape(NX, 240, 128), shape(56, 128, dtype=F32)),
        (keep, other, buffer),
        specs=[whole(48, 128), whole(48, 128), pl.BlockSpec(memory_space=pl.ANY)],
        out_specs=(pl.BlockSpec((NX, 80, 128), lambda n: (0, 2, 0)), whole(56, 128)),
        grid=(1,),
        aliases={2: 0},
    )
    got = lax.all_to_all(buffer, "sx", 0, 0)
    strided, two, one, vol = call(
        functools.partial(last_kernel, out_scale=out_scale, in_scale=in_scale),
        (shape(256, 128), shape(27, 8, C, dtype=F32), shape(27, C, C, dtype=F32), shape(512, 256)),
        (got, two, plane_cols, rows_back, og_rows_back),
    )
    return (
        strided.reshape(8, 8, 4, 128),
        two.reshape(3, 3, 3, 8, C).transpose(3, 4, 0, 1, 2),
        one.reshape(3, 3, 3, C, C).transpose(3, 4, 0, 1, 2),
        vol.reshape(2, C, 8, W),
    )


def solution(mesh):
    return jax.shard_map(
        per_device,
        mesh=mesh,
        in_specs=(P("sx", None, "sy", None), P(), P(), P(), P(None, "sx", "sy", None)),
        out_specs=(
            P(None, "sx", "sy", None),
            P("sx", None, None, None, None),
            P(),
            P("sx", None, "sy", None),
        ),
        check_vma=False,
    )
```

```python
import functools

import jax
import jax.numpy as jnp
from jax import lax
from jax.experimental import pallas as pl
from jax.experimental.pallas import tpu as pltpu
from jax.sharding import PartitionSpec as P

F32 = jnp.float32
BF16 = jnp.bfloat16
NX = 8
NY = 32
C = 32
K = 64
W = 256
CLASSES = ((0, 0), (0, 1), (1, 0), (1, 1))
TAPS = tuple((a, c) for a in range(3) for c in range(3))


def iota(dims, axis):
    return lax.broadcasted_iota(jnp.int32, dims, axis)


def pick(mask):
    return jnp.where(mask, 1.0, 0.0).astype(BF16)


def dot(a, b):
    return jnp.dot(a, b, preferred_element_type=F32)


def move(a, b):
    return dot(a, b).astype(BF16)


def dot_nt(a, b):
    return lax.dot_general(a, b, (((1,), (1,)), ((), ())), preferred_element_type=F32)


def ahead(x, n):
    return jnp.concatenate([x[:, n:], jnp.zeros((x.shape[0], n), x.dtype)], axis=1)


def behind(x, n):
    return jnp.concatenate([jnp.zeros((x.shape[0], n), x.dtype), x[:, :-n]], axis=1)


def step(parity, offset):
    at = parity + offset
    return (1, 1) if at == -1 else (0, 1) if at == 2 else (at, 0)


def variant(pd, pw, da, dc):
    qd, sd = step(pd, da)
    qw, sw = step(pw, dc)
    return ((qd * 2 + qw) * 2 + sd) * 2 + sw


def variants(x, cls):
    move_d = behind if cls[0] else ahead
    move_w = behind if cls[1] else ahead
    along = move_w(x, 1)
    return x, along, move_d(x, 32), move_d(along, 32)


def store_variants(ref, x, cls):
    base = (cls[0] * 2 + cls[1]) * 4
    for n, form in enumerate(variants(x, cls)):
        ref[base + n] = form


def width_block(n):
    flip = lax.rem(lax.axis_index("sy") // 2, 2)
    return n + (1 - 2 * (n % 2)) * flip


def pack_kernel(vol_hbm, og_hbm, out_hbm, vol_ref, og_ref, out_ref, sems):
    copies = (
        pltpu.make_async_copy(vol_hbm, vol_ref, sems.at[0]),
        pltpu.make_async_copy(og_hbm, og_ref, sems.at[1]),
    )
    for copy in copies:
        copy.start()
    row = iota((256, 256), 0)
    col = iota((256, 256), 1)
    by_row = pick(col == (row & 31) * 8 + (row >> 5))
    by_kind = pick(col == ((row >> 3) & 7) * 32 + (row & 7) * 4 + (row >> 6))
    lane = iota((1, 128), 1)
    cls = jnp.where(lane >= 20, 1, 0) + jnp.where(lane >= 40, 1, 0) + jnp.where(lane >= 60, 1, 0)
    u = lane - 20 * cls
    at = iota((128, 128), 0)
    chosen = []
    for j in range(NX):
        w = jnp.where((lane < 80) & (u < 18), 32 * j - 2 + 2 * u + (cls & 1), -1)
        pieces = []
        for pd in range(2):
            from_plane = jnp.where(cls >> 1 == pd, w, -1)
            for block in range(max(0, 32 * j - 2) // 128, min(W - 1, 32 * j + 33) // 128 + 1):
                pieces.append((pd, block, pick(at + 128 * block == from_plane)))
        g = jnp.where((lane >= 80) & (lane < 98), 16 * j - 1 + lane - 80, -1)
        pieces.append((2, 0, pick(at == g)))
        chosen.append(pieces)
    for copy in copies:
        copy.wait()
    planes = (
        move(by_row, vol_ref[0:256]),
        move(by_row, vol_ref[256:512]),
        move(by_kind, og_ref[...]),
    )
    for j in range(NX):
        cat = jnp.concatenate(
            [planes[n][:, block * 128 : (block + 1) * 128] for n, block, _ in chosen[j]], axis=1
        )
        out_ref[j] = move(cat, jnp.concatenate([m for _, _, m in chosen[j]], axis=0))
        copies += (pltpu.make_async_copy(out_ref.at[j], out_hbm.at[width_block(j)], sems.at[2 + j]),)
        copies[-1].start()
    for copy in copies[2:]:
        copy.wait()


def split_kernel(r_ref, cross_ref, pair_ref):
    for s in range(NX):
        cross_ref[s] = r_ref[s, 192:256, :]
        pair_ref[s] = r_ref[s, 0:64, :]


def by_class(parts, cls_cols):
    got = [move(jnp.concatenate(parts[4 * q : 4 * q + 4], axis=1), cls_cols) for q in range(2)]
    return [
        jnp.concatenate([x[:, n * 128 : (n + 1) * 128] for x in got], axis=1) for n in range(4)
    ]


def cotangents(parts, groups, og_cols):
    parts = [x.astype(F32) for x in parts]
    cat = [
        jnp.concatenate(
            [x[g * 64 + e * 8 : g * 64 + e * 8 + 8] for g in range(groups) for x in parts], axis=0
        )
        for e in range(8)
    ]
    return move(jnp.concatenate(cat, axis=1).astype(BF16), og_cols)


def place(strip, offset, width):
    if offset >= width:
        return jnp.zeros((strip.shape[0], width), strip.dtype)
    first = max(0, -offset)
    strip = strip[:, first : min(strip.shape[1], width - offset)]
    offset += first
    parts = [strip]
    if offset:
        parts.insert(0, jnp.zeros((strip.shape[0], offset), strip.dtype))
    rest = width - offset - strip.shape[1]
    if rest:
        parts.append(jnp.zeros((strip.shape[0], rest), strip.dtype))
    return jnp.concatenate(parts, axis=1)


def from_row(rows, target):
    return pick(iota((rows, target.shape[1]), 0) == target)


def kernel_blocks(ref, a, c):
    return [ref[a * 9 + b * 3 + c].astype(F32) for b in range(3)]


def weights_kernel(
    k1_ref, k2_ref, strips_ref, even_ref, odd_ref, cls_ref, og_cols_ref
):
    col = iota((1, 512), 1)
    u = col & 31
    cls_ref[...] = from_row(512, jnp.where(u < 18, ((col >> 5) & 3) * 128 + (col >> 7) * 20 + u, -1))
    col, u = col[:, 0:256], u[:, 0:256]
    og_cols_ref[...] = from_row(1024, jnp.where(u < 18, (col >> 5) * 128 + 80 + u, -1))
    for t, (a, c) in enumerate(TAPS):
        k1 = kernel_blocks(k1_ref, a, c)
        k2 = kernel_blocks(k2_ref, a, c)
        forward = jnp.concatenate(k1, axis=1)
        even = jnp.concatenate([k2[2], k2[0]], axis=1)
        for r in range(4):
            strips_ref[t, r] = place(forward, 32 * r, 256).astype(BF16)
        for r in range(2):
            even_ref[t, r] = place(even, 64 * r, 256).astype(BF16)
            odd_ref[t, r] = place(k2[1], 64 * r, 128).astype(BF16)


def rim_kernel(k1_ref, k2_ref, t1h_ref, t2th_ref):
    gap = jnp.zeros((C, C), F32)
    wide = jnp.zeros((C, K), F32)
    for t, (a, c) in enumerate(TAPS):
        k1 = kernel_blocks(k1_ref, a, c)
        k2 = kernel_blocks(k2_ref, a, c)
        rim = (
            (k1[0], k1[1], gap, gap),
            (gap, k1[0], gap, gap),
            (gap, gap, k1[2], gap),
            (gap, gap, k1[1], k1[2]),
        )
        t1h_ref[:, t * 128 : (t + 1) * 128] = jnp.concatenate(
            [jnp.concatenate(r, axis=1) for r in rim], axis=0
        ).astype(BF16)
        rim = ((k2[2], wide), (wide, wide), (wide, k2[0]), (wide, k2[1]))
        t2th_ref[t] = jnp.concatenate([jnp.concatenate(r, axis=1) for r in rim], axis=0).astype(BF16)


def window(strip, at):
    if at == 0:
        return strip
    none = jnp.zeros((strip.shape[0], 128), strip.dtype)
    return jnp.concatenate([strip[:, 128:], none] if at < 0 else [none, strip[:, :128]], axis=1)


def build_forward(strips_ref, even_ref, odd_ref, t1_ref, t2t_ref):
    none = jnp.zeros((C, 128), BF16)
    for t in range(9):
        for h in range(10):
            at = slice(h * 32, (h + 1) * 32)
            r = (h + 2) % 4
            t1_ref[t, at, :] = window(strips_ref[t, r], (h - 2 - r) // 4)
            if h % 2 == 0:
                r = (h // 2 + 1) % 2
                t2t_ref[t, at, :] = window(even_ref[t, r], (h // 2 - 1 - r) // 2)
            else:
                n = h // 2
                strip = odd_ref[t, n % 2] if n < 4 else none
                t2t_ref[t, at, :] = jnp.concatenate([none, strip] if n > 1 else [strip, none], axis=1)


def build_back(k1_ref, t1t_ref):
    for t, (a, c) in enumerate(TAPS):
        back = jnp.concatenate([x.T for x in reversed(kernel_blocks(k1_ref, a, c))], axis=1)
        for h in range(8):
            t1t_ref[t, h * 32 : (h + 1) * 32, :] = place(back, 32 * h, 320).astype(BF16)


def build_strided(k2_ref, t2_ref):
    for t, (a, c) in enumerate(TAPS):
        strided = jnp.concatenate([x.T for x in kernel_blocks(k2_ref, a, c)], axis=1)
        for g in range(4):
            t2_ref[t, g * 64 : (g + 1) * 64, :] = place(strided, 64 * g, 320).astype(BF16)


def strip_sum(g, blocks, jump):
    width = g.shape[1] // blocks
    total = None
    for n in range(blocks):
        part = g[n * jump : n * jump + 96, n * width : (n + 1) * width]
        total = part if total is None else total + part
    return total


def conv_taps(pd, pw, sign):
    return [(tap, variant(pd, pw, sign * (a - 1), sign * (c - 1))) for tap, (a, c) in enumerate(TAPS)]


def spread_taps(pd, pw):
    depth = ((1, 0),) if pd == 0 else ((2, 0), (0, 1))
    width = ((1, 0),) if pw == 0 else ((2, 0), (0, 1))
    return [(a * 3 + c, sd * 2 + sw) for a, sd in depth for c, sw in width]


def tap_sum(weights_ref, inputs_ref, pairs):
    total = None
    for tap, at in pairs:
        part = dot(weights_ref[tap], inputs_ref[at])
        total = part if total is None else total + part
    return total


def store_cotangents(ref, og):
    along = ahead(og, 1)
    ref[0] = og
    ref[1] = along
    ref[2] = ahead(og, 32)
    ref[3] = ahead(along, 32)


def inner_kernel(
    r_ref, cls_ref, og_cols_ref, strips_ref, even_ref, odd_ref,
    og_ref, xs_ref, pre_ref, grad_ref,
    ogs_ref, t1_ref, t2t_ref,
):
    build_forward(strips_ref, even_ref, odd_ref, t1_ref, t2t_ref)
    parts = [r_ref[s] for s in range(NX)]
    for x, cls in zip(by_class(parts, cls_ref[...]), CLASSES):
        store_variants(xs_ref, x, cls)
    og_ref[...] = cotangents(parts, 4, og_cols_ref[...])
    store_cotangents(ogs_ref, og_ref[...])
    for n, (pd, pw) in enumerate(CLASSES):
        pre_ref[n] = tap_sum(t1_ref, xs_ref, conv_taps(pd, pw, 1))
        grad_ref[n] = tap_sum(t2t_ref, ogs_ref, spread_taps(pd, pw))


def first_kernel(
    xs_ref, pre_ref, ga_ref, og_ref, cross_ref, pair_ref, cls_ref, og_cols_ref, bias_ref, t1h_ref,
    t2th_ref,
    grads_ref, gp_ref, act_ref,
    rim_ref, ogs_ref, own_ref, og_own_ref,
):
    j = width_block(lax.axis_index("sx"))
    t = lax.axis_index("sy")
    low = t > 0
    high = t < NY - 1
    none = jnp.zeros((64, 128), BF16)
    ups = [cross_ref[s] for s in range(NX)]
    downs = [pair_ref[s] for s in range(NX)]
    ups = [jnp.where(low, x, none) for x in ups]
    downs = [jnp.where(high, x, none) for x in downs]
    rims = [jnp.concatenate([x, y], axis=0) for x, y in zip(ups, downs)]
    uses = [
        (n, tap, at) for n, (pd, pw) in enumerate(CLASSES) for tap, at in conv_taps(pd, pw, 1)
    ]
    for n, x in enumerate(by_class(rims, cls_ref[...])):
        forms = variants(x, CLASSES[n])
        for m, tap, at in uses:
            if at // 4 == n:
                rim_ref[m, tap * 128 : (tap + 1) * 128, :] = forms[at % 4]
    store_cotangents(ogs_ref, cotangents(rims, 2, og_cols_ref[...]))

    def with_rim(inner, outer):
        return jnp.concatenate(
            [inner[0:64] + outer[0:64], inner[64:256], inner[256:320] + outer[64:128]], axis=0
        )

    row = lax.broadcasted_iota(jnp.int32, (320, 256), 0)
    u = lax.rem(lax.broadcasted_iota(jnp.int32, (320, 256), 1), 32)
    row_ok = ((row >= 32) | low) & ((row < 288) | high)
    bias = bias_ref[...]
    for n, (pd, pw) in enumerate(CLASSES):
        pre = with_rim(pre_ref[n], dot(t1h_ref[...], rim_ref[n])) + bias
        local = 2 * u + pw
        wide = local + (32 * j - 2)
        ok = row_ok & (local >= 1) & (local <= 34) & (wide >= 0) & (wide < W)
        sigma = jax.nn.sigmoid(pre)
        act_ref[n] = jnp.where(ok, pre * sigma, 0.0).astype(BF16)
        grad = with_rim(ga_ref[n], tap_sum(t2th_ref, ogs_ref, spread_taps(pd, pw)))
        grad = jnp.where(ok, grad * sigma * (1.0 + pre * (1.0 - sigma)), 0.0)
        gp_ref[n] = grad.astype(BF16)
        mine = (u[32:288] >= 1) & (u[32:288] <= 16)
        own_ref[n] = jnp.where(mine, grad[32:288], 0.0).astype(BF16)

    lane = lax.rem(lax.broadcasted_iota(jnp.int32, (256, 256), 1), 32)
    store_cotangents(og_own_ref, jnp.where((lane >= 1) & (lane <= 16), og_ref[...].astype(F32), 0.0).astype(BF16))
    twos, ones = [], []
    for tap, (a, c) in enumerate(TAPS):
        pd, sd = step(0, a - 1)
        pw, sw = step(0, c - 1)
        twos.append(strip_sum(dot_nt(act_ref[pd * 2 + pw], og_own_ref[sd * 2 + sw]), 4, 64))
        g = None
        for n, (pd, pw) in enumerate(CLASSES):
            at = variant(pd, pw, a - 1, c - 1)
            first = tap * 128 + 32
            x = jnp.concatenate(
                [
                    rim_ref[n, first : first + 32, :],
                    xs_ref[at],
                    rim_ref[n, first + 32 : first + 64, :],
                ],
                axis=0,
            )
            part = dot_nt(x, own_ref[n])
            g = part if g is None else g + part
        ones.append(strip_sum(g, 8, 32))
    twos.append(jnp.zeros((32, K), F32))
    ones.append(jnp.zeros((32, C), F32))
    twos = jnp.concatenate(twos, axis=0)
    ones = jnp.concatenate(ones, axis=0)
    twos = [twos[n * 128 : (n + 1) * 128].T for n in range(7)]
    ones = [ones[n * 128 : (n + 1) * 128].T for n in range(7)] + [jnp.zeros((C, 128), F32)] * 3
    for s in range(NX):
        for n in range(12):
            if n < 7:
                tile = twos[n][8 * s : 8 * s + 8]
            else:
                pair = ones[2 * n - 14], ones[2 * n - 13]
                tile = jnp.concatenate([x[4 * s : 4 * s + 4] for x in pair], axis=0)
            grads_ref[s * 2 + n // 6, n % 6 * 8 : n % 6 * 8 + 8, :] = tile


def act_variant(act_ref, a, c):
    pd, sd = step(0, a - 1)
    pw, sw = step(0, c - 1)
    x = act_ref[pd * 2 + pw]
    if sw:
        x = behind(x, 1)
    if sd:
        x = behind(x, 32)
    return x


def strided_kernel(act_ref, k2_ref, out_ref, t2_ref):
    build_strided(k2_ref, t2_ref)
    col = iota((1, 128), 1)
    strided_cols = from_row(256, (col >> 4) * 32 + 1 + (col & 15))
    out = None
    for tap, (a, c) in enumerate(TAPS):
        part = dot(t2_ref[tap], act_variant(act_ref, a, c))
        out = part if out is None else out + part
    out = dot(out.astype(BF16), strided_cols)
    for s in range(NX):
        out_ref[s] = jnp.concatenate(
            [out[g * 64 + 8 * s : g * 64 + 8 * s + 8] for g in range(4)], axis=0
        ).astype(BF16)


def second_kernel(
    gp_ref, k1_ref, strided_ref,
    out_ref, fcol_ref, rows_ref, og_rows_ref,
    gs_ref, t1t_ref,
):
    col = iota((1, 512), 1)
    half = (col >> 6) & 1
    gather_cols = from_row(
        1024, half * 512 + ((col >> 4) & 3) * 128 + (col >> 7) * 32 + 1 + (col & 15)
    )
    fcol_ref[...] = from_row(
        512,
        ((col >> 5) & 3) * 128
        + ((col >> 7) & 1) * 64
        + ((col >> 8) * 2 + (col & 1)) * 16
        + ((col & 31) >> 1),
    )
    row = iota((256, 256), 0)
    col = iota((256, 256), 1)
    rows_ref[...] = pick(col == (row & 7) * 32 + (row >> 3))
    og_rows_ref[...] = pick(col == (row & ~31) + (row & 3) * 8 + ((row >> 2) & 7))
    build_back(k1_ref, t1t_ref)
    for n, cls in enumerate(CLASSES):
        store_variants(gs_ref, gp_ref[n], cls)
    grads = [tap_sum(t1t_ref, gs_ref, conv_taps(pd, pw, -1)).astype(BF16) for pd, pw in CLASSES]
    for q in range(2):
        at = slice(q * 128, (q + 1) * 128)
        cat = jnp.concatenate(
            [grads[n][half * 128 : (half + 1) * 128, at] for half in range(2) for n in range(4)], axis=1
        )
        got = move(cat, gather_cols)
        for e in range(4):
            out_ref[4 * q + e, 0:128, :] = got[:, e * 128 : (e + 1) * 128]
    for s in range(NX):
        out_ref[s, 128:160, :] = strided_ref[s]


def first_sum_kernel(r_ref, out_ref):
    total = r_ref[0]
    for s in range(1, r_ref.shape[0]):
        total = total + r_ref[s]
    out_ref[...] = total


def sum_kernel(r_ref, after_ref, out_ref):
    total = r_ref[0]
    for s in range(1, r_ref.shape[0]):
        total = total + r_ref[s]
    out_ref[...] = total


def pair_kernel(a_ref, b_ref, after_ref, out_ref):
    total = a_ref[...] + b_ref[...]
    for n in range(out_ref.shape[0]):
        out_ref[n] = total


def append_kernel(mine_ref, other_ref, buf_ref, out_ref, two_ref):
    first = lax.rem(lax.axis_index("sy"), 2) == 0
    mine, other = mine_ref[...], other_ref[...]
    even = jnp.where(first, mine, other)
    odd = jnp.where(first, other, mine)
    total = jnp.concatenate([even, odd], axis=0)
    two_ref[...] = total[0:56]
    one = total[56:96]
    hi = one.astype(BF16).astype(F32)
    both = jnp.concatenate([hi, one - hi], axis=0).astype(BF16)
    for s in range(NX):
        out_ref[s] = both


def last_kernel(
    r_ref, g_ref, fcol_ref, rows_ref, og_rows_ref,
    strided_ref, two_ref, one_ref, vol_ref, *, out_scale, in_scale,
):
    halves = []
    for q in range(2):
        cat = jnp.concatenate([r_ref[width_block(4 * q + s), 0:128, :] for s in range(4)], axis=1)
        halves.append(move(cat, fcol_ref[...]))
    for pd in range(2):
        blocks = []
        for half in range(2):
            at = slice((pd * 2 + half) * 128, (pd * 2 + half + 1) * 128)
            blocks.append(jnp.concatenate([halves[0][:, at], halves[1][:, at]], axis=1))
        vol_ref[pd * 256 : (pd + 1) * 256, :] = move(rows_ref[...], jnp.concatenate(blocks, axis=0))
    parts = [r_ref[width_block(s), 128:160, :].astype(F32) for s in range(NX)]
    group = iota((32, 128), 1) >> 4
    blocks = []
    for e in range(8):
        block = None
        for j in range(NX):
            turned = pltpu.roll(parts[j], (j - e) * 16 % 128, 1) if j != e else parts[j]
            block = turned if block is None else jnp.where(group == j, turned, block)
        blocks.append(block)
    strided_ref[...] = move(og_rows_ref[...], jnp.concatenate(blocks, axis=0).astype(BF16))
    sums = [r_ref[s, 160:200, :].astype(F32) + r_ref[s, 200:240, :].astype(F32) for s in range(NX)]
    two = g_ref[...] * out_scale
    for n in range(7):
        one = jnp.concatenate([x[4 * n : 4 * n + 4] for x in sums], axis=0) * in_scale
        for m in range(4 * n, min(4 * n + 4, 27)):
            a, c = TAPS[m // 3]
            tap = a * 9 + m % 3 * 3 + c
            at = slice((m - 4 * n) * 32, (m - 4 * n + 1) * 32)
            one_ref[tap] = one[:, at]
            two_ref[tap] = two[n * 8 : (n + 1) * 8, at]


def call(body, outs, args, scratch=(), specs=None, out_specs=None, aliases=None, grid=(), us=1, vmem=16):
    return pl.pallas_call(
        body,
        out_shape=outs,
        grid=grid,
        in_specs=specs or [pl.BlockSpec(memory_space=pltpu.VMEM)] * len(args),
        out_specs=out_specs or jax.tree.map(lambda _: pl.BlockSpec(memory_space=pltpu.VMEM), outs),
        scratch_shapes=list(scratch),
        input_output_aliases=aliases or {},
        compiler_params=pltpu.CompilerParams(vmem_limit_bytes=vmem * 1024 * 1024),
        cost_estimate=pl.CostEstimate(flops=us * 10**9, bytes_accessed=0, transcendentals=0),
    )(*args)


def whole(*dims):
    return pl.BlockSpec(dims, lambda n: (0,) * len(dims))


def shape(*dims, dtype=BF16):
    return jax.ShapeDtypeStruct(dims, dtype)


def per_device(volume, kernel_one, bias_one, kernel_two, out_grad):
    out_scale = (8 * 128 * 128) ** (-0.5)
    in_scale = (16 * 256 * 256) ** (-0.5)
    chunks = call(
        pack_kernel,
        shape(NX, 256, 128),
        (volume.reshape(512, 256), out_grad.reshape(256, 128)),
        specs=[pl.BlockSpec(memory_space=pl.ANY)] * 2,
        out_specs=pl.BlockSpec(memory_space=pl.ANY),
        scratch=(
            pltpu.VMEM((512, 256), BF16),
            pltpu.VMEM((256, 128), BF16),
            pltpu.VMEM((NX, 256, 128), BF16),
            pltpu.SemaphoreType.DMA((2 + NX,)),
        ),
        vmem=60,
    )
    got = lax.all_to_all(chunks, "sx", 0, 0)
    k1 = kernel_one.transpose(2, 3, 4, 0, 1).reshape(27, C, C)
    k2 = kernel_two.transpose(2, 3, 4, 1, 0).reshape(27, C, K)
    strips, even, odd, class_cols, og_cols = call(
        weights_kernel,
        (
            shape(9, 4, 32, 256), shape(9, 2, 32, 256), shape(9, 2, 32, 128),
            shape(512, 512), shape(1024, 256),
        ),
        (k1, k2),
        us=3,
    )
    bias = jnp.tile(bias_one.astype(F32), 10)[:, None]
    cross, pair = call(split_kernel, (shape(NX, 64, 128), shape(NX, 64, 128)), (got,))
    k1, k2, cross = lax.optimization_barrier((k1, k2, cross))
    t1h, t2th = call(rim_kernel, (shape(128, 9 * 128), shape(9, 128, 128)), (k1, k2))
    up = [
        (s * NY + t, (s ^ (t % 2)) * NY + (t + 1) % NY) for s in range(NX) for t in range(NY)
    ]
    cross = lax.ppermute(cross, ("sx", "sy"), up)
    pair = lax.ppermute(pair, ("sx", "sy"), [(b, a) for a, b in up])
    og, xs, pre, grad_act = call(
        inner_kernel,
        (shape(256, 256), shape(16, 256, 256), shape(4, 320, 256, dtype=F32), shape(4, 320, 256, dtype=F32)),
        (got, class_cols, og_cols, strips, even, odd),
        scratch=(
            pltpu.VMEM((4, 256, 256), BF16),
            pltpu.VMEM((9, 320, 256), BF16),
            pltpu.VMEM((9, 320, 256), BF16),
        ),
        us=5,
    )
    grads, gp, act = call(
        first_kernel,
        (shape(2 * NX, 48, 128, dtype=F32), shape(4, 320, 256), shape(4, 320, 256)),
        (xs, pre, grad_act, og, cross, pair, class_cols, og_cols, bias, t1h, t2th),
        scratch=(
            pltpu.VMEM((4, 9 * 128, 256), BF16),
            pltpu.VMEM((4, 128, 256), BF16),
            pltpu.VMEM((4, 256, 256), BF16),
            pltpu.VMEM((4, 256, 256), BF16),
        ),
        us=5,
    )
    grads = lax.all_to_all(
        grads,
        ("sx", "sy"),
        0,
        0,
        axis_index_groups=[
            [s * NY + 2 * q + r for s in range(NX) for r in range(2)] for q in range(NY // 2)
        ],
    )
    both = [pl.BlockSpec(memory_space=pltpu.VMEM), pl.BlockSpec(memory_space=pl.ANY)]
    keep = call(first_sum_kernel, shape(48, 128, dtype=F32), (grads,))
    keep, act = lax.optimization_barrier((keep, act))
    other = lax.ppermute(keep, "sy", [(i, i ^ 2) for i in range(NY)])
    strided = call(
        strided_kernel,
        shape(NX, 32, 128),
        (act, k2),
        scratch=(pltpu.VMEM((9, 256, 320), BF16),),
        us=2,
    )
    keep = call(
        pair_kernel,
        shape(8, 48, 128, dtype=F32),
        (keep, other, strided),
        specs=[pl.BlockSpec(memory_space=pltpu.VMEM)] + both,
    )
    keep, gp = lax.optimization_barrier((keep, gp))
    buffer, plane_cols, rows_back, og_rows_back = call(
        second_kernel,
        (shape(NX, 240, 128), shape(512, 512), shape(256, 256), shape(256, 256)),
        (gp, k1, strided),
        scratch=(pltpu.VMEM((16, 320, 256), BF16), pltpu.VMEM((9, 256, 320), BF16)),
        us=5,
        vmem=20,
    )
    keep = lax.all_to_all(
        keep,
        "sy",
        0,
        0,
        axis_index_groups=[[4 * z + r for z in (4, 0, 5, 1, 6, 2, 7, 3)] for r in range(4)],
    )
    keep = call(sum_kernel, shape(48, 128, dtype=F32), (keep, buffer), specs=both)
    other = lax.ppermute(keep, "sy", [(i, i ^ 1) for i in range(NY)])
    buffer, two = call(
        append_kernel,
        (shape(NX, 240, 128), shape(56, 128, dtype=F32)),
        (keep, other, buffer),
        specs=[whole(48, 128), whole(48, 128), pl.BlockSpec(memory_space=pl.ANY)],
        out_specs=(pl.BlockSpec((NX, 80, 128), lambda n: (0, 2, 0)), whole(56, 128)),
        grid=(1,),
        aliases={2: 0},
    )
    got = lax.all_to_all(buffer, "sx", 0, 0)
    strided, two, one, vol = call(
        functools.partial(last_kernel, out_scale=out_scale, in_scale=in_scale),
        (shape(256, 128), shape(27, 8, C, dtype=F32), shape(27, C, C, dtype=F32), shape(512, 256)),
        (got, two, plane_cols, rows_back, og_rows_back),
    )
    return (
        strided.reshape(8, 8, 4, 128),
        two.reshape(3, 3, 3, 8, C).transpose(3, 4, 0, 1, 2),
        one.reshape(3, 3, 3, C, C).transpose(3, 4, 0, 1, 2),
        vol.reshape(2, C, 8, W),
    )


def solution(mesh):
    return jax.shard_map(
        per_device,
        mesh=mesh,
        in_specs=(P("sx", None, "sy", None), P(), P(), P(), P(None, "sx", "sy", None)),
        out_specs=(
            P(None, "sx", "sy", None),
            P("sx", None, None, None, None),
            P(),
            P("sx", None, "sy", None),
        ),
        check_vma=False,
    )
```

```python
import functools

import jax
import jax.numpy as jnp
from jax import lax
from jax.experimental import pallas as pl
from jax.experimental.pallas import tpu as pltpu
from jax.sharding import PartitionSpec as P

F32 = jnp.float32
BF16 = jnp.bfloat16
NX = 8
NY = 32
C = 32
K = 64
W = 256
CLASSES = ((0, 0), (0, 1), (1, 0), (1, 1))
ORDER = (4, 5, 0, 1, 6, 7, 2, 3)
PLACE = tuple(ORDER.index(s) for s in range(NX))
TAPS = tuple((a, c) for a in range(3) for c in range(3))


def iota(dims, axis):
    return lax.broadcasted_iota(jnp.int32, dims, axis)


def pick(mask):
    return jnp.where(mask, 1.0, 0.0).astype(BF16)


def dot(a, b):
    return jnp.dot(a, b, preferred_element_type=F32)


def move(a, b):
    return dot(a, b).astype(BF16)


def dot_nt(a, b):
    return lax.dot_general(a, b, (((1,), (1,)), ((), ())), preferred_element_type=F32)


def ahead(x, n):
    return jnp.concatenate([x[:, n:], jnp.zeros((x.shape[0], n), x.dtype)], axis=1)


def behind(x, n):
    return jnp.concatenate([jnp.zeros((x.shape[0], n), x.dtype), x[:, :-n]], axis=1)


def step(parity, offset):
    at = parity + offset
    return (1, 1) if at == -1 else (0, 1) if at == 2 else (at, 0)


def variant(pd, pw, da, dc):
    qd, sd = step(pd, da)
    qw, sw = step(pw, dc)
    return ((qd * 2 + qw) * 2 + sd) * 2 + sw


def variants(x, cls):
    move_d = behind if cls[0] else ahead
    move_w = behind if cls[1] else ahead
    along = move_w(x, 1)
    return x, along, move_d(x, 32), move_d(along, 32)


def store_variants(ref, x, cls):
    base = (cls[0] * 2 + cls[1]) * 4
    for n, form in enumerate(variants(x, cls)):
        ref[base + n] = form


def width_block(n):
    flip = lax.rem(lax.axis_index("sy") // 2, 2)
    return n + (1 - 2 * (n % 2)) * flip


def pack_kernel(vol_hbm, og_hbm, out_hbm, vol_ref, og_ref, out_ref, sems):
    copies = (
        pltpu.make_async_copy(vol_hbm, vol_ref, sems.at[0]),
        pltpu.make_async_copy(og_hbm, og_ref, sems.at[1]),
    )
    for copy in copies:
        copy.start()
    row = iota((256, 256), 0)
    col = iota((256, 256), 1)
    by_row = pick(col == (row & 31) * 8 + (row >> 5))
    by_kind = pick(col == ((row >> 3) & 7) * 32 + (row & 7) * 4 + (row >> 6))
    lane = iota((1, 128), 1)
    cls = jnp.where(lane >= 20, 1, 0) + jnp.where(lane >= 40, 1, 0) + jnp.where(lane >= 60, 1, 0)
    u = lane - 20 * cls
    at = iota((128, 128), 0)
    chosen = []
    for j in range(NX):
        w = jnp.where((lane < 80) & (u < 18), 32 * j - 2 + 2 * u + (cls & 1), -1)
        pieces = []
        for pd in range(2):
            from_plane = jnp.where(cls >> 1 == pd, w, -1)
            for block in range(max(0, 32 * j - 2) // 128, min(W - 1, 32 * j + 33) // 128 + 1):
                pieces.append((pd, block, pick(at + 128 * block == from_plane)))
        g = jnp.where((lane >= 80) & (lane < 98), 16 * j - 1 + lane - 80, -1)
        pieces.append((2, 0, pick(at == g)))
        chosen.append(pieces)
    for copy in copies:
        copy.wait()
    planes = (
        move(by_row, vol_ref[0:256]),
        move(by_row, vol_ref[256:512]),
        move(by_kind, og_ref[...]),
    )
    for j in range(NX):
        cat = jnp.concatenate(
            [planes[n][:, block * 128 : (block + 1) * 128] for n, block, _ in chosen[j]], axis=1
        )
        out_ref[j] = move(cat, jnp.concatenate([m for _, _, m in chosen[j]], axis=0))
        copies += (pltpu.make_async_copy(out_ref.at[j], out_hbm.at[width_block(j)], sems.at[2 + j]),)
        copies[-1].start()
    for copy in copies[2:]:
        copy.wait()


def split_kernel(r_ref, cross_ref, pair_ref):
    for s in range(NX):
        cross_ref[s] = r_ref[s, 192:256, :]
        pair_ref[s] = r_ref[s, 0:64, :]


def by_class(parts, cls_cols):
    got = [move(jnp.concatenate(parts[4 * q : 4 * q + 4], axis=1), cls_cols) for q in range(2)]
    return [
        jnp.concatenate([x[:, n * 128 : (n + 1) * 128] for x in got], axis=1) for n in range(4)
    ]


def cotangents(parts, groups, og_cols):
    parts = [x.astype(F32) for x in parts]
    cat = [
        jnp.concatenate(
            [x[g * 64 + e * 8 : g * 64 + e * 8 + 8] for g in range(groups) for x in parts], axis=0
        )
        for e in range(8)
    ]
    return move(jnp.concatenate(cat, axis=1).astype(BF16), og_cols)


def place(strip, offset, width):
    if offset >= width:
        return jnp.zeros((strip.shape[0], width), strip.dtype)
    first = max(0, -offset)
    strip = strip[:, first : min(strip.shape[1], width - offset)]
    offset += first
    parts = [strip]
    if offset:
        parts.insert(0, jnp.zeros((strip.shape[0], offset), strip.dtype))
    rest = width - offset - strip.shape[1]
    if rest:
        parts.append(jnp.zeros((strip.shape[0], rest), strip.dtype))
    return jnp.concatenate(parts, axis=1)


def from_row(rows, target):
    return pick(iota((rows, target.shape[1]), 0) == target)


def kernel_blocks(ref, a, c):
    return [ref[a * 9 + b * 3 + c].astype(F32) for b in range(3)]


def weights_kernel(
    k1_ref, k2_ref, strips_ref, even_ref, odd_ref, cls_ref, og_cols_ref
):
    col = iota((1, 512), 1)
    u = col & 31
    cls_ref[...] = from_row(512, jnp.where(u < 18, ((col >> 5) & 3) * 128 + (col >> 7) * 20 + u, -1))
    col, u = col[:, 0:256], u[:, 0:256]
    og_cols_ref[...] = from_row(1024, jnp.where(u < 18, (col >> 5) * 128 + 80 + u, -1))
    for t, (a, c) in enumerate(TAPS):
        k1 = kernel_blocks(k1_ref, a, c)
        k2 = kernel_blocks(k2_ref, a, c)
        forward = jnp.concatenate(k1, axis=1)
        even = jnp.concatenate([k2[2], k2[0]], axis=1)
        for r in range(4):
            strips_ref[t, r] = place(forward, 32 * r, 256).astype(BF16)
        for r in range(2):
            even_ref[t, r] = place(even, 64 * r, 256).astype(BF16)
            odd_ref[t, r] = place(k2[1], 64 * r, 128).astype(BF16)


def rim_kernel(k1_ref, k2_ref, t1h_ref, t2th_ref):
    gap = jnp.zeros((C, C), F32)
    wide = jnp.zeros((C, K), F32)
    for t, (a, c) in enumerate(TAPS):
        k1 = kernel_blocks(k1_ref, a, c)
        k2 = kernel_blocks(k2_ref, a, c)
        rim = (
            (k1[0], k1[1], gap, gap),
            (gap, k1[0], gap, gap),
            (gap, gap, k1[2], gap),
            (gap, gap, k1[1], k1[2]),
        )
        t1h_ref[:, t * 128 : (t + 1) * 128] = jnp.concatenate(
            [jnp.concatenate(r, axis=1) for r in rim], axis=0
        ).astype(BF16)
        rim = ((k2[2], wide), (wide, wide), (wide, k2[0]), (wide, k2[1]))
        t2th_ref[t] = jnp.concatenate([jnp.concatenate(r, axis=1) for r in rim], axis=0).astype(BF16)


def window(strip, at):
    if at == 0:
        return strip
    none = jnp.zeros((strip.shape[0], 128), strip.dtype)
    return jnp.concatenate([strip[:, 128:], none] if at < 0 else [none, strip[:, :128]], axis=1)


def build_forward(strips_ref, even_ref, odd_ref, t1_ref, t2t_ref):
    none = jnp.zeros((C, 128), BF16)
    for t in range(9):
        for h in range(10):
            at = slice(h * 32, (h + 1) * 32)
            r = (h + 2) % 4
            t1_ref[t, at, :] = window(strips_ref[t, r], (h - 2 - r) // 4)
            if h % 2 == 0:
                r = (h // 2 + 1) % 2
                t2t_ref[t, at, :] = window(even_ref[t, r], (h // 2 - 1 - r) // 2)
            else:
                n = h // 2
                strip = odd_ref[t, n % 2] if n < 4 else none
                t2t_ref[t, at, :] = jnp.concatenate([none, strip] if n > 1 else [strip, none], axis=1)


def build_back(k1_ref, t1t_ref):
    for t, (a, c) in enumerate(TAPS):
        back = jnp.concatenate([x.T for x in reversed(kernel_blocks(k1_ref, a, c))], axis=1)
        for h in range(8):
            t1t_ref[t, h * 32 : (h + 1) * 32, :] = place(back, 32 * h, 320).astype(BF16)


def build_strided(k2_ref, t2_ref):
    for t, (a, c) in enumerate(TAPS):
        strided = jnp.concatenate([x.T for x in kernel_blocks(k2_ref, a, c)], axis=1)
        for g in range(4):
            t2_ref[t, g * 64 : (g + 1) * 64, :] = place(strided, 64 * g, 320).astype(BF16)


def strip_sum(g, blocks, jump):
    width = g.shape[1] // blocks
    total = None
    for n in range(blocks):
        part = g[n * jump : n * jump + 96, n * width : (n + 1) * width]
        total = part if total is None else total + part
    return total


def conv_taps(pd, pw, sign):
    return [(tap, variant(pd, pw, sign * (a - 1), sign * (c - 1))) for tap, (a, c) in enumerate(TAPS)]


def spread_taps(pd, pw):
    depth = ((1, 0),) if pd == 0 else ((2, 0), (0, 1))
    width = ((1, 0),) if pw == 0 else ((2, 0), (0, 1))
    return [(a * 3 + c, sd * 2 + sw) for a, sd in depth for c, sw in width]


def tap_sum(weights_ref, inputs_ref, pairs):
    total = None
    for tap, at in pairs:
        part = dot(weights_ref[tap], inputs_ref[at])
        total = part if total is None else total + part
    return total


def store_cotangents(ref, og):
    along = ahead(og, 1)
    ref[0] = og
    ref[1] = along
    ref[2] = ahead(og, 32)
    ref[3] = ahead(along, 32)


def inner_kernel(
    r_ref, cls_ref, og_cols_ref, strips_ref, even_ref, odd_ref,
    og_ref, xs_ref, pre_ref, grad_ref,
    ogs_ref, t1_ref, t2t_ref,
):
    build_forward(strips_ref, even_ref, odd_ref, t1_ref, t2t_ref)
    parts = [r_ref[s] for s in range(NX)]
    for x, cls in zip(by_class(parts, cls_ref[...]), CLASSES):
        store_variants(xs_ref, x, cls)
    og_ref[...] = cotangents(parts, 4, og_cols_ref[...])
    store_cotangents(ogs_ref, og_ref[...])
    for n, (pd, pw) in enumerate(CLASSES):
        pre_ref[n] = tap_sum(t1_ref, xs_ref, conv_taps(pd, pw, 1))
        grad_ref[n] = tap_sum(t2t_ref, ogs_ref, spread_taps(pd, pw))


def first_kernel(
    xs_ref, pre_ref, ga_ref, og_ref, cross_ref, pair_ref, cls_ref, og_cols_ref, bias_ref, t1h_ref,
    t2th_ref,
    grads_ref, gp_ref, act_ref,
    rim_ref, ogs_ref, own_ref, og_own_ref,
):
    j = width_block(lax.axis_index("sx"))
    t = lax.axis_index("sy")
    low = t > 0
    high = t < NY - 1
    none = jnp.zeros((64, 128), BF16)
    ups = [cross_ref[s] for s in range(NX)]
    downs = [pair_ref[s] for s in range(NX)]
    ups = [jnp.where(low, x, none) for x in ups]
    downs = [jnp.where(high, x, none) for x in downs]
    rims = [jnp.concatenate([x, y], axis=0) for x, y in zip(ups, downs)]
    uses = [
        (n, tap, at) for n, (pd, pw) in enumerate(CLASSES) for tap, at in conv_taps(pd, pw, 1)
    ]
    for n, x in enumerate(by_class(rims, cls_ref[...])):
        forms = variants(x, CLASSES[n])
        for m, tap, at in uses:
            if at // 4 == n:
                rim_ref[m, tap * 128 : (tap + 1) * 128, :] = forms[at % 4]
    store_cotangents(ogs_ref, cotangents(rims, 2, og_cols_ref[...]))

    def with_rim(inner, outer):
        return jnp.concatenate(
            [inner[0:64] + outer[0:64], inner[64:256], inner[256:320] + outer[64:128]], axis=0
        )

    row = lax.broadcasted_iota(jnp.int32, (320, 256), 0)
    u = lax.rem(lax.broadcasted_iota(jnp.int32, (320, 256), 1), 32)
    row_ok = ((row >= 32) | low) & ((row < 288) | high)
    bias = bias_ref[...]
    for n, (pd, pw) in enumerate(CLASSES):
        pre = with_rim(pre_ref[n], dot(t1h_ref[...], rim_ref[n])) + bias
        local = 2 * u + pw
        wide = local + (32 * j - 2)
        ok = row_ok & (local >= 1) & (local <= 34) & (wide >= 0) & (wide < W)
        sigma = jax.nn.sigmoid(pre)
        act_ref[n] = jnp.where(ok, pre * sigma, 0.0).astype(BF16)
        grad = with_rim(ga_ref[n], tap_sum(t2th_ref, ogs_ref, spread_taps(pd, pw)))
        grad = jnp.where(ok, grad * sigma * (1.0 + pre * (1.0 - sigma)), 0.0)
        gp_ref[n] = grad.astype(BF16)
        mine = (u[32:288] >= 1) & (u[32:288] <= 16)
        own_ref[n] = jnp.where(mine, grad[32:288], 0.0).astype(BF16)

    lane = lax.rem(lax.broadcasted_iota(jnp.int32, (256, 256), 1), 32)
    store_cotangents(og_own_ref, jnp.where((lane >= 1) & (lane <= 16), og_ref[...].astype(F32), 0.0).astype(BF16))
    twos, ones = [], []
    for tap, (a, c) in enumerate(TAPS):
        pd, sd = step(0, a - 1)
        pw, sw = step(0, c - 1)
        twos.append(strip_sum(dot_nt(act_ref[pd * 2 + pw], og_own_ref[sd * 2 + sw]), 4, 64))
        g = None
        for n, (pd, pw) in enumerate(CLASSES):
            at = variant(pd, pw, a - 1, c - 1)
            first = tap * 128 + 32
            x = jnp.concatenate(
                [
                    rim_ref[n, first : first + 32, :],
                    xs_ref[at],
                    rim_ref[n, first + 32 : first + 64, :],
                ],
                axis=0,
            )
            part = dot_nt(x, own_ref[n])
            g = part if g is None else g + part
        ones.append(strip_sum(g, 8, 32))
    twos.append(jnp.zeros((32, K), F32))
    ones.append(jnp.zeros((32, C), F32))
    twos = jnp.concatenate(twos, axis=0)
    ones = jnp.concatenate(ones, axis=0)
    twos = [twos[n * 128 : (n + 1) * 128].T for n in range(7)]
    ones = [ones[n * 128 : (n + 1) * 128].T for n in range(7)] + [jnp.zeros((C, 128), F32)] * 3
    for s in range(NX):
        for n in range(12):
            if n < 7:
                tile = twos[n][8 * s : 8 * s + 8]
            else:
                pair = ones[2 * n - 14], ones[2 * n - 13]
                tile = jnp.concatenate([x[4 * s : 4 * s + 4] for x in pair], axis=0)
            grads_ref[s * 2 + n // 6, n % 6 * 8 : n % 6 * 8 + 8, :] = tile


def act_variant(act_ref, a, c):
    pd, sd = step(0, a - 1)
    pw, sw = step(0, c - 1)
    x = act_ref[pd * 2 + pw]
    if sw:
        x = behind(x, 1)
    if sd:
        x = behind(x, 32)
    return x


def strided_kernel(act_ref, k2_ref, out_ref, t2_ref):
    build_strided(k2_ref, t2_ref)
    col = iota((1, 128), 1)
    strided_cols = from_row(256, (col >> 4) * 32 + 1 + (col & 15))
    out = None
    for tap, (a, c) in enumerate(TAPS):
        part = dot(t2_ref[tap], act_variant(act_ref, a, c))
        out = part if out is None else out + part
    out = dot(out.astype(BF16), strided_cols)
    for s in range(NX):
        out_ref[s] = jnp.concatenate(
            [out[g * 64 + 8 * s : g * 64 + 8 * s + 8] for g in range(4)], axis=0
        ).astype(BF16)


def second_kernel(
    gp_ref, k1_ref, strided_ref,
    out_ref, fcol_ref, rows_ref, og_rows_ref,
    gs_ref, t1t_ref,
):
    col = iota((1, 512), 1)
    half = (col >> 6) & 1
    gather_cols = from_row(
        1024, half * 512 + ((col >> 4) & 3) * 128 + (col >> 7) * 32 + 1 + (col & 15)
    )
    fcol_ref[...] = from_row(
        512,
        ((col >> 5) & 3) * 128
        + ((col >> 7) & 1) * 64
        + ((col >> 8) * 2 + (col & 1)) * 16
        + ((col & 31) >> 1),
    )
    row = iota((256, 256), 0)
    col = iota((256, 256), 1)
    rows_ref[...] = pick(col == (row & 7) * 32 + (row >> 3))
    og_rows_ref[...] = pick(col == (row & ~31) + (row & 3) * 8 + ((row >> 2) & 7))
    build_back(k1_ref, t1t_ref)
    for n, cls in enumerate(CLASSES):
        store_variants(gs_ref, gp_ref[n], cls)
    grads = [tap_sum(t1t_ref, gs_ref, conv_taps(pd, pw, -1)).astype(BF16) for pd, pw in CLASSES]
    for q in range(2):
        at = slice(q * 128, (q + 1) * 128)
        cat = jnp.concatenate(
            [grads[n][half * 128 : (half + 1) * 128, at] for half in range(2) for n in range(4)], axis=1
        )
        got = move(cat, gather_cols)
        for e in range(4):
            out_ref[PLACE[4 * q + e], 0:128, :] = got[:, e * 128 : (e + 1) * 128]
    for s in range(NX):
        out_ref[PLACE[s], 128:160, :] = strided_ref[s]


def first_sum_kernel(r_ref, out_ref):
    total = r_ref[0]
    for s in range(1, r_ref.shape[0]):
        total = total + r_ref[s]
    out_ref[...] = total


def sum_kernel(r_ref, after_ref, out_ref):
    total = r_ref[0]
    for s in range(1, r_ref.shape[0]):
        total = total + r_ref[s]
    out_ref[...] = total


def pair_kernel(a_ref, b_ref, after_ref, out_ref):
    total = a_ref[...] + b_ref[...]
    for n in range(out_ref.shape[0]):
        out_ref[n] = total


def append_kernel(mine_ref, other_ref, buf_ref, out_ref, two_ref):
    first = lax.rem(lax.axis_index("sy"), 2) == 0
    mine, other = mine_ref[...], other_ref[...]
    even = jnp.where(first, mine, other)
    odd = jnp.where(first, other, mine)
    total = jnp.concatenate([even, odd], axis=0)
    two_ref[...] = total[0:56]
    one = total[56:96]
    hi = one.astype(BF16).astype(F32)
    both = jnp.concatenate([hi, one - hi], axis=0).astype(BF16)
    for s in range(NX):
        out_ref[s] = both


def last_kernel(
    r_ref, g_ref, fcol_ref, rows_ref, og_rows_ref,
    strided_ref, two_ref, one_ref, vol_ref, *, out_scale, in_scale,
):
    halves = []
    for q in range(2):
        cat = jnp.concatenate([r_ref[width_block(PLACE[4 * q + s]), 0:128, :] for s in range(4)], axis=1)
        halves.append(move(cat, fcol_ref[...]))
    for pd in range(2):
        blocks = []
        for half in range(2):
            at = slice((pd * 2 + half) * 128, (pd * 2 + half + 1) * 128)
            blocks.append(jnp.concatenate([halves[0][:, at], halves[1][:, at]], axis=1))
        vol_ref[pd * 256 : (pd + 1) * 256, :] = move(rows_ref[...], jnp.concatenate(blocks, axis=0))
    parts = [r_ref[width_block(PLACE[s]), 128:160, :].astype(F32) for s in range(NX)]
    group = iota((32, 128), 1) >> 4
    blocks = []
    for e in range(8):
        block = None
        for j in range(NX):
            turned = pltpu.roll(parts[j], (j - e) * 16 % 128, 1) if j != e else parts[j]
            block = turned if block is None else jnp.where(group == j, turned, block)
        blocks.append(block)
    strided_ref[...] = move(og_rows_ref[...], jnp.concatenate(blocks, axis=0).astype(BF16))
    sums = [r_ref[s, 160:200, :].astype(F32) + r_ref[s, 200:240, :].astype(F32) for s in PLACE]
    two = g_ref[...] * out_scale
    for n in range(7):
        one = jnp.concatenate([x[4 * n : 4 * n + 4] for x in sums], axis=0) * in_scale
        for m in range(4 * n, min(4 * n + 4, 27)):
            a, c = TAPS[m // 3]
            tap = a * 9 + m % 3 * 3 + c
            at = slice((m - 4 * n) * 32, (m - 4 * n + 1) * 32)
            one_ref[tap] = one[:, at]
            two_ref[tap] = two[n * 8 : (n + 1) * 8, at]


def call(body, outs, args, scratch=(), specs=None, out_specs=None, aliases=None, grid=(), us=1, vmem=16):
    return pl.pallas_call(
        body,
        out_shape=outs,
        grid=grid,
        in_specs=specs or [pl.BlockSpec(memory_space=pltpu.VMEM)] * len(args),
        out_specs=out_specs or jax.tree.map(lambda _: pl.BlockSpec(memory_space=pltpu.VMEM), outs),
        scratch_shapes=list(scratch),
        input_output_aliases=aliases or {},
        compiler_params=pltpu.CompilerParams(vmem_limit_bytes=vmem * 1024 * 1024),
        cost_estimate=pl.CostEstimate(flops=us * 10**9, bytes_accessed=0, transcendentals=0),
    )(*args)


def whole(*dims):
    return pl.BlockSpec(dims, lambda n: (0,) * len(dims))


def shape(*dims, dtype=BF16):
    return jax.ShapeDtypeStruct(dims, dtype)


def per_device(volume, kernel_one, bias_one, kernel_two, out_grad):
    out_scale = (8 * 128 * 128) ** (-0.5)
    in_scale = (16 * 256 * 256) ** (-0.5)
    chunks = call(
        pack_kernel,
        shape(NX, 256, 128),
        (volume.reshape(512, 256), out_grad.reshape(256, 128)),
        specs=[pl.BlockSpec(memory_space=pl.ANY)] * 2,
        out_specs=pl.BlockSpec(memory_space=pl.ANY),
        scratch=(
            pltpu.VMEM((512, 256), BF16),
            pltpu.VMEM((256, 128), BF16),
            pltpu.VMEM((NX, 256, 128), BF16),
            pltpu.SemaphoreType.DMA((2 + NX,)),
        ),
        vmem=60,
    )
    got = lax.all_to_all(chunks, "sx", 0, 0)
    k1 = kernel_one.transpose(2, 3, 4, 0, 1).reshape(27, C, C)
    k2 = kernel_two.transpose(2, 3, 4, 1, 0).reshape(27, C, K)
    strips, even, odd, class_cols, og_cols = call(
        weights_kernel,
        (
            shape(9, 4, 32, 256), shape(9, 2, 32, 256), shape(9, 2, 32, 128),
            shape(512, 512), shape(1024, 256),
        ),
        (k1, k2),
        us=3,
    )
    bias = jnp.tile(bias_one.astype(F32), 10)[:, None]
    cross, pair = call(split_kernel, (shape(NX, 64, 128), shape(NX, 64, 128)), (got,))
    k1, k2, cross = lax.optimization_barrier((k1, k2, cross))
    t1h, t2th = call(rim_kernel, (shape(128, 9 * 128), shape(9, 128, 128)), (k1, k2))
    up = [
        (s * NY + t, (s ^ (t % 2)) * NY + (t + 1) % NY) for s in range(NX) for t in range(NY)
    ]
    cross = lax.ppermute(cross, ("sx", "sy"), up)
    pair = lax.ppermute(pair, ("sx", "sy"), [(b, a) for a, b in up])
    og, xs, pre, grad_act = call(
        inner_kernel,
        (shape(256, 256), shape(16, 256, 256), shape(4, 320, 256, dtype=F32), shape(4, 320, 256, dtype=F32)),
        (got, class_cols, og_cols, strips, even, odd),
        scratch=(
            pltpu.VMEM((4, 256, 256), BF16),
            pltpu.VMEM((9, 320, 256), BF16),
            pltpu.VMEM((9, 320, 256), BF16),
        ),
        us=5,
    )
    grads, gp, act = call(
        first_kernel,
        (shape(2 * NX, 48, 128, dtype=F32), shape(4, 320, 256), shape(4, 320, 256)),
        (xs, pre, grad_act, og, cross, pair, class_cols, og_cols, bias, t1h, t2th),
        scratch=(
            pltpu.VMEM((4, 9 * 128, 256), BF16),
            pltpu.VMEM((4, 128, 256), BF16),
            pltpu.VMEM((4, 256, 256), BF16),
            pltpu.VMEM((4, 256, 256), BF16),
        ),
        us=5,
    )
    grads = lax.all_to_all(
        grads,
        ("sx", "sy"),
        0,
        0,
        axis_index_groups=[
            [s * NY + 2 * q + r for s in range(NX) for r in range(2)] for q in range(NY // 2)
        ],
    )
    both = [pl.BlockSpec(memory_space=pltpu.VMEM), pl.BlockSpec(memory_space=pl.ANY)]
    keep = call(first_sum_kernel, shape(48, 128, dtype=F32), (grads,))
    keep, act = lax.optimization_barrier((keep, act))
    other = lax.ppermute(keep, "sy", [(i, i ^ 2) for i in range(NY)])
    strided = call(
        strided_kernel,
        shape(NX, 32, 128),
        (act, k2),
        scratch=(pltpu.VMEM((9, 256, 320), BF16),),
        us=2,
    )
    keep = call(
        pair_kernel,
        shape(8, 48, 128, dtype=F32),
        (keep, other, strided),
        specs=[pl.BlockSpec(memory_space=pltpu.VMEM)] + both,
    )
    keep, gp = lax.optimization_barrier((keep, gp))
    buffer, plane_cols, rows_back, og_rows_back = call(
        second_kernel,
        (shape(NX, 240, 128), shape(512, 512), shape(256, 256), shape(256, 256)),
        (gp, k1, strided),
        scratch=(pltpu.VMEM((16, 320, 256), BF16), pltpu.VMEM((9, 256, 320), BF16)),
        us=5,
        vmem=20,
    )
    keep = lax.all_to_all(
        keep,
        "sy",
        0,
        0,
        axis_index_groups=[[4 * z + r for z in (4, 0, 5, 1, 6, 2, 7, 3)] for r in range(4)],
    )
    keep = call(sum_kernel, shape(48, 128, dtype=F32), (keep, buffer), specs=both)
    other = lax.ppermute(keep, "sy", [(i, i ^ 1) for i in range(NY)])
    buffer, two = call(
        append_kernel,
        (shape(NX, 240, 128), shape(56, 128, dtype=F32)),
        (keep, other, buffer),
        specs=[whole(48, 128), whole(48, 128), pl.BlockSpec(memory_space=pl.ANY)],
        out_specs=(pl.BlockSpec((NX, 80, 128), lambda n: (0, 2, 0)), whole(56, 128)),
        grid=(1,),
        aliases={2: 0},
    )
    got = lax.all_to_all(buffer, "sx", 0, 0, axis_index_groups=[list(ORDER)])
    strided, two, one, vol = call(
        functools.partial(last_kernel, out_scale=out_scale, in_scale=in_scale),
        (shape(256, 128), shape(27, 8, C, dtype=F32), shape(27, C, C, dtype=F32), shape(512, 256)),
        (got, two, plane_cols, rows_back, og_rows_back),
    )
    return (
        strided.reshape(8, 8, 4, 128),
        two.reshape(3, 3, 3, 8, C).transpose(3, 4, 0, 1, 2),
        one.reshape(3, 3, 3, C, C).transpose(3, 4, 0, 1, 2),
        vol.reshape(2, C, 8, W),
    )


def solution(mesh):
    return jax.shard_map(
        per_device,
        mesh=mesh,
        in_specs=(P("sx", None, "sy", None), P(), P(), P(), P(None, "sx", "sy", None)),
        out_specs=(
            P(None, "sx", "sy", None),
            P("sx", None, None, None, None),
            P(),
            P("sx", None, "sy", None),
        ),
        check_vma=False,
    )
```

```python
import functools

import jax
import jax.numpy as jnp
from jax import lax
from jax.experimental import pallas as pl
from jax.experimental.pallas import tpu as pltpu
from jax.sharding import PartitionSpec as P

F32 = jnp.float32
BF16 = jnp.bfloat16
NX = 8
NY = 32
C = 32
K = 64
W = 256
CLASSES = ((0, 0), (0, 1), (1, 0), (1, 1))
ORDER = (4, 5, 0, 1, 6, 7, 2, 3)
PLACE = tuple(ORDER.index(s) for s in range(NX))
TAPS = tuple((a, c) for a in range(3) for c in range(3))


def iota(dims, axis):
    return lax.broadcasted_iota(jnp.int32, dims, axis)


def pick(mask):
    return jnp.where(mask, 1.0, 0.0).astype(BF16)


def dot(a, b):
    return jnp.dot(a, b, preferred_element_type=F32)


def move(a, b):
    return dot(a, b).astype(BF16)


def dot_nt(a, b):
    return lax.dot_general(a, b, (((1,), (1,)), ((), ())), preferred_element_type=F32)


def ahead(x, n):
    return jnp.concatenate([x[:, n:], jnp.zeros((x.shape[0], n), x.dtype)], axis=1)


def behind(x, n):
    return jnp.concatenate([jnp.zeros((x.shape[0], n), x.dtype), x[:, :-n]], axis=1)


def step(parity, offset):
    at = parity + offset
    return (1, 1) if at == -1 else (0, 1) if at == 2 else (at, 0)


def variant(pd, pw, da, dc):
    qd, sd = step(pd, da)
    qw, sw = step(pw, dc)
    return ((qd * 2 + qw) * 2 + sd) * 2 + sw


def variants(x, cls):
    move_d = behind if cls[0] else ahead
    move_w = behind if cls[1] else ahead
    along = move_w(x, 1)
    return x, along, move_d(x, 32), move_d(along, 32)


def store_variants(ref, x, cls):
    base = (cls[0] * 2 + cls[1]) * 4
    for n, form in enumerate(variants(x, cls)):
        ref[base + n] = form


def width_block(n):
    flip = lax.rem(lax.axis_index("sy") // 2, 2)
    return n + (1 - 2 * (n % 2)) * flip


def pack_kernel(vol_hbm, og_hbm, out_hbm, vol_ref, og_ref, out_ref, sems):
    copies = (
        pltpu.make_async_copy(vol_hbm, vol_ref, sems.at[0]),
        pltpu.make_async_copy(og_hbm, og_ref, sems.at[1]),
    )
    for copy in copies:
        copy.start()
    row = iota((256, 256), 0)
    col = iota((256, 256), 1)
    by_row = pick(col == (row & 31) * 8 + (row >> 5))
    by_kind = pick(col == ((row >> 3) & 7) * 32 + (row & 7) * 4 + (row >> 6))
    lane = iota((1, 128), 1)
    cls = jnp.where(lane >= 20, 1, 0) + jnp.where(lane >= 40, 1, 0) + jnp.where(lane >= 60, 1, 0)
    u = lane - 20 * cls
    at = iota((128, 128), 0)
    chosen = []
    for j in range(NX):
        w = jnp.where((lane < 80) & (u < 18), 32 * j - 2 + 2 * u + (cls & 1), -1)
        pieces = []
        for pd in range(2):
            from_plane = jnp.where(cls >> 1 == pd, w, -1)
            for block in range(max(0, 32 * j - 2) // 128, min(W - 1, 32 * j + 33) // 128 + 1):
                pieces.append((pd, block, pick(at + 128 * block == from_plane)))
        g = jnp.where((lane >= 80) & (lane < 98), 16 * j - 1 + lane - 80, -1)
        pieces.append((2, 0, pick(at == g)))
        chosen.append(pieces)
    for copy in copies:
        copy.wait()
    planes = (
        move(by_row, vol_ref[0:256]),
        move(by_row, vol_ref[256:512]),
        move(by_kind, og_ref[...]),
    )
    for j in range(NX):
        cat = jnp.concatenate(
            [planes[n][:, block * 128 : (block + 1) * 128] for n, block, _ in chosen[j]], axis=1
        )
        out_ref[j] = move(cat, jnp.concatenate([m for _, _, m in chosen[j]], axis=0))
        copies += (pltpu.make_async_copy(out_ref.at[j], out_hbm.at[width_block(j)], sems.at[2 + j]),)
        copies[-1].start()
    for copy in copies[2:]:
        copy.wait()


def split_kernel(r_ref, cross_ref, pair_ref):
    for s in range(NX):
        cross_ref[s] = r_ref[s, 192:256, :]
        pair_ref[s] = r_ref[s, 0:64, :]


def by_class(parts, cls_cols):
    got = [move(jnp.concatenate(parts[4 * q : 4 * q + 4], axis=1), cls_cols) for q in range(2)]
    return [
        jnp.concatenate([x[:, n * 128 : (n + 1) * 128] for x in got], axis=1) for n in range(4)
    ]


def cotangents(parts, groups, og_cols):
    parts = [x.astype(F32) for x in parts]
    cat = [
        jnp.concatenate(
            [x[g * 64 + e * 8 : g * 64 + e * 8 + 8] for g in range(groups) for x in parts], axis=0
        )
        for e in range(8)
    ]
    return move(jnp.concatenate(cat, axis=1).astype(BF16), og_cols)


def place(strip, offset, width):
    if offset >= width:
        return jnp.zeros((strip.shape[0], width), strip.dtype)
    first = max(0, -offset)
    strip = strip[:, first : min(strip.shape[1], width - offset)]
    offset += first
    parts = [strip]
    if offset:
        parts.insert(0, jnp.zeros((strip.shape[0], offset), strip.dtype))
    rest = width - offset - strip.shape[1]
    if rest:
        parts.append(jnp.zeros((strip.shape[0], rest), strip.dtype))
    return jnp.concatenate(parts, axis=1)


def from_row(rows, target):
    return pick(iota((rows, target.shape[1]), 0) == target)


def kernel_blocks(ref, a, c):
    return [ref[a * 9 + b * 3 + c].astype(F32) for b in range(3)]


def weights_kernel(
    k1_ref, k2_ref, strips_ref, even_ref, odd_ref, cls_ref, og_cols_ref
):
    col = iota((1, 512), 1)
    u = col & 31
    cls_ref[...] = from_row(512, jnp.where(u < 18, ((col >> 5) & 3) * 128 + (col >> 7) * 20 + u, -1))
    col, u = col[:, 0:256], u[:, 0:256]
    og_cols_ref[...] = from_row(1024, jnp.where(u < 18, (col >> 5) * 128 + 80 + u, -1))
    for t, (a, c) in enumerate(TAPS):
        k1 = kernel_blocks(k1_ref, a, c)
        k2 = kernel_blocks(k2_ref, a, c)
        forward = jnp.concatenate(k1, axis=1)
        even = jnp.concatenate([k2[2], k2[0]], axis=1)
        for r in range(4):
            strips_ref[t, r] = place(forward, 32 * r, 256).astype(BF16)
        for r in range(2):
            even_ref[t, r] = place(even, 64 * r, 256).astype(BF16)
            odd_ref[t, r] = place(k2[1], 64 * r, 128).astype(BF16)


def rim_kernel(k1_ref, k2_ref, t1h_ref, t2th_ref):
    gap = jnp.zeros((C, C), F32)
    wide = jnp.zeros((C, K), F32)
    for t, (a, c) in enumerate(TAPS):
        k1 = kernel_blocks(k1_ref, a, c)
        k2 = kernel_blocks(k2_ref, a, c)
        rim = (
            (k1[0], k1[1], gap, gap),
            (gap, k1[0], gap, gap),
            (gap, gap, k1[2], gap),
            (gap, gap, k1[1], k1[2]),
        )
        t1h_ref[:, t * 128 : (t + 1) * 128] = jnp.concatenate(
            [jnp.concatenate(r, axis=1) for r in rim], axis=0
        ).astype(BF16)
        rim = ((k2[2], wide), (wide, wide), (wide, k2[0]), (wide, k2[1]))
        t2th_ref[t] = jnp.concatenate([jnp.concatenate(r, axis=1) for r in rim], axis=0).astype(BF16)


def window(strip, at):
    if at == 0:
        return strip
    none = jnp.zeros((strip.shape[0], 128), strip.dtype)
    return jnp.concatenate([strip[:, 128:], none] if at < 0 else [none, strip[:, :128]], axis=1)


def build_forward(strips_ref, even_ref, odd_ref, t1_ref, t2t_ref):
    none = jnp.zeros((C, 128), BF16)
    for t in range(9):
        for h in range(10):
            at = slice(h * 32, (h + 1) * 32)
            r = (h + 2) % 4
            t1_ref[t, at, :] = window(strips_ref[t, r], (h - 2 - r) // 4)
            if h % 2 == 0:
                r = (h // 2 + 1) % 2
                t2t_ref[t, at, :] = window(even_ref[t, r], (h // 2 - 1 - r) // 2)
            else:
                n = h // 2
                strip = odd_ref[t, n % 2] if n < 4 else none
                t2t_ref[t, at, :] = jnp.concatenate([none, strip] if n > 1 else [strip, none], axis=1)


def build_back(k1_ref, t1t_ref):
    for t, (a, c) in enumerate(TAPS):
        back = jnp.concatenate([x.T for x in reversed(kernel_blocks(k1_ref, a, c))], axis=1)
        for h in range(8):
            t1t_ref[t, h * 32 : (h + 1) * 32, :] = place(back, 32 * h, 320).astype(BF16)


def build_strided(k2_ref, t2_ref):
    for t, (a, c) in enumerate(TAPS):
        strided = jnp.concatenate([x.T for x in kernel_blocks(k2_ref, a, c)], axis=1)
        for g in range(4):
            t2_ref[t, g * 64 : (g + 1) * 64, :] = place(strided, 64 * g, 320).astype(BF16)


def strip_sum(g, blocks, jump):
    width = g.shape[1] // blocks
    total = None
    for n in range(blocks):
        part = g[n * jump : n * jump + 96, n * width : (n + 1) * width]
        total = part if total is None else total + part
    return total


def conv_taps(pd, pw, sign):
    return [(tap, variant(pd, pw, sign * (a - 1), sign * (c - 1))) for tap, (a, c) in enumerate(TAPS)]


def spread_taps(pd, pw):
    depth = ((1, 0),) if pd == 0 else ((2, 0), (0, 1))
    width = ((1, 0),) if pw == 0 else ((2, 0), (0, 1))
    return [(a * 3 + c, sd * 2 + sw) for a, sd in depth for c, sw in width]


def tap_sum(weights_ref, inputs_ref, pairs):
    total = None
    for tap, at in pairs:
        part = dot(weights_ref[tap], inputs_ref[at])
        total = part if total is None else total + part
    return total


def store_cotangents(ref, og):
    along = ahead(og, 1)
    ref[0] = og
    ref[1] = along
    ref[2] = ahead(og, 32)
    ref[3] = ahead(along, 32)


def inner_kernel(
    r_ref, cls_ref, og_cols_ref, strips_ref, even_ref, odd_ref,
    og_ref, xs_ref, pre_ref, grad_ref,
    ogs_ref, t1_ref, t2t_ref,
):
    build_forward(strips_ref, even_ref, odd_ref, t1_ref, t2t_ref)
    parts = [r_ref[s] for s in range(NX)]
    for x, cls in zip(by_class(parts, cls_ref[...]), CLASSES):
        store_variants(xs_ref, x, cls)
    og_ref[...] = cotangents(parts, 4, og_cols_ref[...])
    store_cotangents(ogs_ref, og_ref[...])
    for n, (pd, pw) in enumerate(CLASSES):
        pre_ref[n] = tap_sum(t1_ref, xs_ref, conv_taps(pd, pw, 1))
        grad_ref[n] = tap_sum(t2t_ref, ogs_ref, spread_taps(pd, pw))


def first_kernel(
    xs_ref, pre_ref, ga_ref, og_ref, cross_ref, pair_ref, cls_ref, og_cols_ref, bias_ref, t1h_ref,
    t2th_ref,
    grads_ref, gp_ref, act_ref,
    rim_ref, ogs_ref, own_ref, og_own_ref,
):
    j = width_block(lax.axis_index("sx"))
    t = lax.axis_index("sy")
    low = t > 0
    high = t < NY - 1
    none = jnp.zeros((64, 128), BF16)
    ups = [cross_ref[s] for s in range(NX)]
    downs = [pair_ref[s] for s in range(NX)]
    ups = [jnp.where(low, x, none) for x in ups]
    downs = [jnp.where(high, x, none) for x in downs]
    rims = [jnp.concatenate([x, y], axis=0) for x, y in zip(ups, downs)]
    uses = [
        (n, tap, at) for n, (pd, pw) in enumerate(CLASSES) for tap, at in conv_taps(pd, pw, 1)
    ]
    for n, x in enumerate(by_class(rims, cls_ref[...])):
        forms = variants(x, CLASSES[n])
        for m, tap, at in uses:
            if at // 4 == n:
                rim_ref[m, tap * 128 : (tap + 1) * 128, :] = forms[at % 4]
    store_cotangents(ogs_ref, cotangents(rims, 2, og_cols_ref[...]))

    def with_rim(inner, outer):
        return jnp.concatenate(
            [inner[0:64] + outer[0:64], inner[64:256], inner[256:320] + outer[64:128]], axis=0
        )

    row = lax.broadcasted_iota(jnp.int32, (320, 256), 0)
    u = lax.rem(lax.broadcasted_iota(jnp.int32, (320, 256), 1), 32)
    row_ok = ((row >= 32) | low) & ((row < 288) | high)
    bias = bias_ref[...]
    for n, (pd, pw) in enumerate(CLASSES):
        pre = with_rim(pre_ref[n], dot(t1h_ref[...], rim_ref[n])) + bias
        local = 2 * u + pw
        wide = local + (32 * j - 2)
        ok = row_ok & (local >= 1) & (local <= 34) & (wide >= 0) & (wide < W)
        sigma = jax.nn.sigmoid(pre)
        act_ref[n] = jnp.where(ok, pre * sigma, 0.0).astype(BF16)
        grad = with_rim(ga_ref[n], tap_sum(t2th_ref, ogs_ref, spread_taps(pd, pw)))
        grad = jnp.where(ok, grad * sigma * (1.0 + pre * (1.0 - sigma)), 0.0)
        gp_ref[n] = grad.astype(BF16)
        mine = (u[32:288] >= 1) & (u[32:288] <= 16)
        own_ref[n] = jnp.where(mine, grad[32:288], 0.0).astype(BF16)

    lane = lax.rem(lax.broadcasted_iota(jnp.int32, (256, 256), 1), 32)
    store_cotangents(og_own_ref, jnp.where((lane >= 1) & (lane <= 16), og_ref[...].astype(F32), 0.0).astype(BF16))
    twos, ones = [], []
    for tap, (a, c) in enumerate(TAPS):
        pd, sd = step(0, a - 1)
        pw, sw = step(0, c - 1)
        twos.append(strip_sum(dot_nt(act_ref[pd * 2 + pw], og_own_ref[sd * 2 + sw]), 4, 64))
        g = None
        for n, (pd, pw) in enumerate(CLASSES):
            at = variant(pd, pw, a - 1, c - 1)
            first = tap * 128 + 32
            x = jnp.concatenate(
                [
                    rim_ref[n, first : first + 32, :],
                    xs_ref[at],
                    rim_ref[n, first + 32 : first + 64, :],
                ],
                axis=0,
            )
            part = dot_nt(x, own_ref[n])
            g = part if g is None else g + part
        ones.append(strip_sum(g, 8, 32))
    twos.append(jnp.zeros((32, K), F32))
    ones.append(jnp.zeros((32, C), F32))
    twos = jnp.concatenate(twos, axis=0)
    ones = jnp.concatenate(ones, axis=0)
    twos = [twos[n * 128 : (n + 1) * 128].T for n in range(7)]
    ones = [ones[n * 128 : (n + 1) * 128].T for n in range(7)] + [jnp.zeros((C, 128), F32)] * 3
    for s in range(NX):
        for n in range(12):
            if n < 7:
                tile = twos[n][8 * s : 8 * s + 8]
            else:
                pair = ones[2 * n - 14], ones[2 * n - 13]
                tile = jnp.concatenate([x[4 * s : 4 * s + 4] for x in pair], axis=0)
            grads_ref[s * 2 + n // 6, n % 6 * 8 : n % 6 * 8 + 8, :] = tile


def act_variant(act_ref, a, c):
    pd, sd = step(0, a - 1)
    pw, sw = step(0, c - 1)
    x = act_ref[pd * 2 + pw]
    if sw:
        x = behind(x, 1)
    if sd:
        x = behind(x, 32)
    return x


def strided_kernel(act_ref, k2_ref, out_ref, t2_ref):
    build_strided(k2_ref, t2_ref)
    col = iota((1, 128), 1)
    strided_cols = from_row(256, (col >> 4) * 32 + 1 + (col & 15))
    out = None
    for tap, (a, c) in enumerate(TAPS):
        part = dot(t2_ref[tap], act_variant(act_ref, a, c))
        out = part if out is None else out + part
    out = dot(out.astype(BF16), strided_cols)
    for s in range(NX):
        out_ref[s] = jnp.concatenate(
            [out[g * 64 + 8 * s : g * 64 + 8 * s + 8] for g in range(4)], axis=0
        ).astype(BF16)


def second_kernel(
    gp_ref, k1_ref, strided_ref,
    out_ref, fcol_ref, rows_ref, og_rows_ref,
    gs_ref, t1t_ref,
):
    col = iota((1, 512), 1)
    half = (col >> 6) & 1
    gather_cols = from_row(
        1024, half * 512 + ((col >> 4) & 3) * 128 + (col >> 7) * 32 + 1 + (col & 15)
    )
    fcol_ref[...] = from_row(
        512,
        ((col >> 5) & 3) * 128
        + ((col >> 7) & 1) * 64
        + ((col >> 8) * 2 + (col & 1)) * 16
        + ((col & 31) >> 1),
    )
    row = iota((256, 256), 0)
    col = iota((256, 256), 1)
    rows_ref[...] = pick(col == (row & 7) * 32 + (row >> 3))
    og_rows_ref[...] = pick(col == (row & ~31) + (row & 3) * 8 + ((row >> 2) & 7))
    build_back(k1_ref, t1t_ref)
    for n, cls in enumerate(CLASSES):
        store_variants(gs_ref, gp_ref[n], cls)
    grads = [tap_sum(t1t_ref, gs_ref, conv_taps(pd, pw, -1)).astype(BF16) for pd, pw in CLASSES]
    for q in range(2):
        at = slice(q * 128, (q + 1) * 128)
        cat = jnp.concatenate(
            [grads[n][half * 128 : (half + 1) * 128, at] for half in range(2) for n in range(4)], axis=1
        )
        got = move(cat, gather_cols)
        for e in range(4):
            out_ref[PLACE[4 * q + e], 0:128, :] = got[:, e * 128 : (e + 1) * 128]
    for s in range(NX):
        out_ref[PLACE[s], 128:160, :] = strided_ref[s]


def first_sum_kernel(r_ref, out_ref):
    total = r_ref[0]
    for s in range(1, r_ref.shape[0]):
        total = total + r_ref[s]
    out_ref[...] = total


def sum_kernel(r_ref, after_ref, out_ref):
    total = r_ref[0]
    for s in range(1, r_ref.shape[0]):
        total = total + r_ref[s]
    out_ref[...] = total


def pair_kernel(a_ref, b_ref, after_ref, out_ref):
    total = a_ref[...] + b_ref[...]
    for n in range(out_ref.shape[0]):
        out_ref[n] = total


def append_kernel(mine_ref, other_ref, buf_ref, out_ref, two_ref):
    first = lax.rem(lax.axis_index("sy"), 2) == 0
    mine, other = mine_ref[...], other_ref[...]
    even = jnp.where(first, mine, other)
    odd = jnp.where(first, other, mine)
    total = jnp.concatenate([even, odd], axis=0)
    two_ref[...] = total[0:56]
    one = total[56:96]
    hi = one.astype(BF16).astype(F32)
    both = jnp.concatenate([hi, one - hi], axis=0).astype(BF16)
    for s in range(NX):
        out_ref[s] = both


def last_kernel(
    r_ref, g_ref, fcol_ref, rows_ref, og_rows_ref,
    strided_ref, two_ref, one_ref, vol_ref, *, out_scale, in_scale,
):
    halves = []
    for q in range(2):
        cat = jnp.concatenate([r_ref[width_block(PLACE[4 * q + s]), 0:128, :] for s in range(4)], axis=1)
        halves.append(move(cat, fcol_ref[...]))
    for pd in range(2):
        blocks = []
        for half in range(2):
            at = slice((pd * 2 + half) * 128, (pd * 2 + half + 1) * 128)
            blocks.append(jnp.concatenate([halves[0][:, at], halves[1][:, at]], axis=1))
        vol_ref[pd * 256 : (pd + 1) * 256, :] = move(rows_ref[...], jnp.concatenate(blocks, axis=0))
    parts = [r_ref[width_block(PLACE[s]), 128:160, :].astype(F32) for s in range(NX)]
    group = iota((32, 128), 1) >> 4
    blocks = []
    for e in range(8):
        block = None
        for j in range(NX):
            turned = pltpu.roll(parts[j], (j - e) * 16 % 128, 1) if j != e else parts[j]
            block = turned if block is None else jnp.where(group == j, turned, block)
        blocks.append(block)
    strided_ref[...] = move(og_rows_ref[...], jnp.concatenate(blocks, axis=0).astype(BF16))
    sums = [r_ref[s, 160:240, :].astype(F32) for s in PLACE]
    sums = [x[0:40] + x[40:80] for x in sums]
    two = g_ref[...] * out_scale
    for n in range(7):
        one = jnp.concatenate([x[4 * n : 4 * n + 4] for x in sums], axis=0) * in_scale
        for m in range(4 * n, min(4 * n + 4, 27)):
            a, c = TAPS[m // 3]
            tap = a * 9 + m % 3 * 3 + c
            at = slice((m - 4 * n) * 32, (m - 4 * n + 1) * 32)
            one_ref[tap] = one[:, at]
            two_ref[tap] = two[n * 8 : (n + 1) * 8, at]


def call(body, outs, args, scratch=(), specs=None, out_specs=None, aliases=None, grid=(), us=1, vmem=16):
    return pl.pallas_call(
        body,
        out_shape=outs,
        grid=grid,
        in_specs=specs or [pl.BlockSpec(memory_space=pltpu.VMEM)] * len(args),
        out_specs=out_specs or jax.tree.map(lambda _: pl.BlockSpec(memory_space=pltpu.VMEM), outs),
        scratch_shapes=list(scratch),
        input_output_aliases=aliases or {},
        compiler_params=pltpu.CompilerParams(vmem_limit_bytes=vmem * 1024 * 1024),
        cost_estimate=pl.CostEstimate(flops=us * 10**9, bytes_accessed=0, transcendentals=0),
    )(*args)


def whole(*dims):
    return pl.BlockSpec(dims, lambda n: (0,) * len(dims))


def shape(*dims, dtype=BF16):
    return jax.ShapeDtypeStruct(dims, dtype)


def per_device(volume, kernel_one, bias_one, kernel_two, out_grad):
    out_scale = (8 * 128 * 128) ** (-0.5)
    in_scale = (16 * 256 * 256) ** (-0.5)
    chunks = call(
        pack_kernel,
        shape(NX, 256, 128),
        (volume.reshape(512, 256), out_grad.reshape(256, 128)),
        specs=[pl.BlockSpec(memory_space=pl.ANY)] * 2,
        out_specs=pl.BlockSpec(memory_space=pl.ANY),
        scratch=(
            pltpu.VMEM((512, 256), BF16),
            pltpu.VMEM((256, 128), BF16),
            pltpu.VMEM((NX, 256, 128), BF16),
            pltpu.SemaphoreType.DMA((2 + NX,)),
        ),
        vmem=60,
    )
    got = lax.all_to_all(chunks, "sx", 0, 0)
    k1 = kernel_one.transpose(2, 3, 4, 0, 1).reshape(27, C, C)
    k2 = kernel_two.transpose(2, 3, 4, 1, 0).reshape(27, C, K)
    strips, even, odd, class_cols, og_cols = call(
        weights_kernel,
        (
            shape(9, 4, 32, 256), shape(9, 2, 32, 256), shape(9, 2, 32, 128),
            shape(512, 512), shape(1024, 256),
        ),
        (k1, k2),
        us=3,
    )
    bias = jnp.tile(bias_one.astype(F32), 10)[:, None]
    cross, pair = call(split_kernel, (shape(NX, 64, 128), shape(NX, 64, 128)), (got,))
    k1, k2, cross = lax.optimization_barrier((k1, k2, cross))
    t1h, t2th = call(rim_kernel, (shape(128, 9 * 128), shape(9, 128, 128)), (k1, k2))
    up = [
        (s * NY + t, (s ^ (t % 2)) * NY + (t + 1) % NY) for s in range(NX) for t in range(NY)
    ]
    cross = lax.ppermute(cross, ("sx", "sy"), up)
    pair = lax.ppermute(pair, ("sx", "sy"), [(b, a) for a, b in up])
    og, xs, pre, grad_act = call(
        inner_kernel,
        (shape(256, 256), shape(16, 256, 256), shape(4, 320, 256, dtype=F32), shape(4, 320, 256, dtype=F32)),
        (got, class_cols, og_cols, strips, even, odd),
        scratch=(
            pltpu.VMEM((4, 256, 256), BF16),
            pltpu.VMEM((9, 320, 256), BF16),
            pltpu.VMEM((9, 320, 256), BF16),
        ),
        us=5,
    )
    grads, gp, act = call(
        first_kernel,
        (shape(2 * NX, 48, 128, dtype=F32), shape(4, 320, 256), shape(4, 320, 256)),
        (xs, pre, grad_act, og, cross, pair, class_cols, og_cols, bias, t1h, t2th),
        scratch=(
            pltpu.VMEM((4, 9 * 128, 256), BF16),
            pltpu.VMEM((4, 128, 256), BF16),
            pltpu.VMEM((4, 256, 256), BF16),
            pltpu.VMEM((4, 256, 256), BF16),
        ),
        us=5,
    )
    grads = lax.all_to_all(
        grads,
        ("sx", "sy"),
        0,
        0,
        axis_index_groups=[
            [s * NY + 2 * q + r for s in range(NX) for r in range(2)] for q in range(NY // 2)
        ],
    )
    both = [pl.BlockSpec(memory_space=pltpu.VMEM), pl.BlockSpec(memory_space=pl.ANY)]
    keep = call(first_sum_kernel, shape(48, 128, dtype=F32), (grads,))
    keep, act = lax.optimization_barrier((keep, act))
    other = lax.ppermute(keep, "sy", [(i, i ^ 2) for i in range(NY)])
    strided = call(
        strided_kernel,
        shape(NX, 32, 128),
        (act, k2),
        scratch=(pltpu.VMEM((9, 256, 320), BF16),),
        us=2,
    )
    keep = call(
        pair_kernel,
        shape(8, 48, 128, dtype=F32),
        (keep, other, strided),
        specs=[pl.BlockSpec(memory_space=pltpu.VMEM)] + both,
    )
    keep, gp = lax.optimization_barrier((keep, gp))
    buffer, plane_cols, rows_back, og_rows_back = call(
        second_kernel,
        (shape(NX, 240, 128), shape(512, 512), shape(256, 256), shape(256, 256)),
        (gp, k1, strided),
        scratch=(pltpu.VMEM((16, 320, 256), BF16), pltpu.VMEM((9, 256, 320), BF16)),
        us=5,
        vmem=20,
    )
    keep = lax.all_to_all(
        keep,
        "sy",
        0,
        0,
        axis_index_groups=[[4 * z + r for z in (4, 0, 5, 1, 6, 2, 7, 3)] for r in range(4)],
    )
    keep = call(sum_kernel, shape(48, 128, dtype=F32), (keep, buffer), specs=both)
    other = lax.ppermute(keep, "sy", [(i, i ^ 1) for i in range(NY)])
    buffer, two = call(
        append_kernel,
        (shape(NX, 240, 128), shape(56, 128, dtype=F32)),
        (keep, other, buffer),
        specs=[whole(48, 128), whole(48, 128), pl.BlockSpec(memory_space=pl.ANY)],
        out_specs=(pl.BlockSpec((NX, 80, 128), lambda n: (0, 2, 0)), whole(56, 128)),
        grid=(1,),
        aliases={2: 0},
    )
    got = lax.all_to_all(buffer, "sx", 0, 0, axis_index_groups=[list(ORDER)])
    strided, two, one, vol = call(
        functools.partial(last_kernel, out_scale=out_scale, in_scale=in_scale),
        (shape(256, 128), shape(27, 8, C, dtype=F32), shape(27, C, C, dtype=F32), shape(512, 256)),
        (got, two, plane_cols, rows_back, og_rows_back),
    )
    return (
        strided.reshape(8, 8, 4, 128),
        two.reshape(3, 3, 3, 8, C).transpose(3, 4, 0, 1, 2),
        one.reshape(3, 3, 3, C, C).transpose(3, 4, 0, 1, 2),
        vol.reshape(2, C, 8, W),
    )


def solution(mesh):
    return jax.shard_map(
        per_device,
        mesh=mesh,
        in_specs=(P("sx", None, "sy", None), P(), P(), P(), P(None, "sx", "sy", None)),
        out_specs=(
            P(None, "sx", "sy", None),
            P("sx", None, None, None, None),
            P(),
            P("sx", None, "sy", None),
        ),
        check_vma=False,
    )
```
